32 devices in a mesh: groups: 2 (over x), blk: 16 (over z, y, core).
Axes of the slice: x: 2, y: 2, z: 4, core: 2. Of those that a mesh axis runs over, the one named last changes fastest.
Arguments:
- features: bfloat16 [8192, 512], P(('groups', 'blk')), parts along dimension 0, may hold values from -6 to 6
- tiles: bfloat16 [1536, 128, 128], P(('groups', 'blk')), parts along dimension 0, may hold values from -0.1875 to 0.1875
- block_rows: int32 [1536], P(('groups', 'blk')), parts along dimension 0, may hold values from 0 to 1, as said below
- block_cols: int32 [1536], P(('groups', 'blk')), parts along dimension 0, may hold values from 0 to 31
- block_count: int32 [32], P(('groups', 'blk')), parts along dimension 0, may hold values from 8 to 48, as said below
- ln_gain: float32 [512], replicated, may hold values from 0.1 to 1.9
- w_msg: bfloat16 [512, 512], replicated, may hold values from -0.25 to 0.25
- w_query: bfloat16 [512, 512], replicated, may hold values from -0.25 to 0.25
- w_key: bfloat16 [512, 512], replicated, may hold values from -0.25 to 0.25
- w_value: bfloat16 [512, 512], replicated, may hold values from -0.25 to 0.25
- w_gate: bfloat16 [512, 512], replicated, may hold values from -0.25 to 0.25
- w_out: bfloat16 [512, 512], replicated, may hold values from -0.25 to 0.25
- omega: float32 [64, 128], replicated, may hold values from -4 to 4
- ln2_gain: float32 [512], replicated, may hold values from 0.1 to 1.9
- w_up: bfloat16 [512, 1024], replicated, may hold values from -0.25 to 0.25
- w_down: bfloat16 [1024, 512], replicated, may hold values from -0.1875 to 0.1875
Outputs:
- updated: bfloat16 [8192, 512], P(('groups', 'blk')), parts along dimension 0
The draws below stay inside these ranges and needn't reach their ends.
There are 2 independent parts, one for each index of `groups`. The reference program is written for one: setup_inputs(seed, part) draws one part's arguments, and reference() takes and returns one part's arrays. A program takes and returns all parts, laid end to end along the dimension named above; an argument that names none is the same for every part. Nothing has to cross between parts.
Inputs may be any that keep to these rules, and one draw needn't show every extreme that they name: `block_count`: in every draw exactly one device of each part uses all 48 slots; the others use 48 // 6 to 24. `block_rows`: no two slots of one device name the same row block and column block.
All inputs are finite; a program needn't handle non-finite values.
Results may differ from the reference program's by a relative error of at most 0.0055.
Values may be sent and summed in bfloat16 or wider, within the bound.
No kernel may reach another device: no remote copies, remote signals or barrier semaphores. Data moves between devices by JAX's collectives and lax.ppermute only.
A program may use at most 128 MiB of HBM per device.

```python
import jax
import jax.numpy as jnp
from jax import lax

D = 512
HEADS = 8
FFN = 1024
FEAT = 128
TILE = 128
MAXB = 48
NODE_DEV = 256
HDIM = 64
NODES = 4096
SLOTS = 768
RB = 2
NCB = 32
N_BLK = 16


def slot_pairs(key):
    key = jax.random.fold_in(key, 11)
    keys = jax.random.split(key, N_BLK)
    picks = jax.vmap(lambda sub: jax.random.permutation(sub, RB * NCB)[:MAXB])(keys)
    return picks.reshape(N_BLK * MAXB).astype(jnp.int32)


def draw_block_rows(key, part):
    return (slot_pairs(key) // NCB).astype(jnp.int32)


def draw_block_cols(key, part):
    return (slot_pairs(key) % NCB).astype(jnp.int32)


def draw_block_count(key, part):
    key = jax.random.fold_in(key, 7)
    first, second = jax.random.split(key)
    counts = jax.random.randint(first, (N_BLK,), MAXB // 6, MAXB // 2 + 1).astype(jnp.int32)
    busy = jax.random.randint(second, (), 0, N_BLK)
    return counts.at[busy].set(MAXB).astype(jnp.int32)


def levels(own_key, extent, shards, least, top_value):
    loudness, own = 1.0, jax.random.fold_in(own_key, 6)
    for dim, parts in shards:
        steps = jnp.exp(jax.random.uniform(jax.random.fold_in(own, dim), (parts,), jnp.float32, least / len(shards), top_value / len(shards)))
        loudness = loudness * jnp.repeat(steps, extent[dim] // parts).reshape([-1 if axis == dim else 1 for axis in range(len(extent))])
    return loudness


def bell_draw(stream_key, extent, scale, limit, cuts=(), kind=jnp.bfloat16):
    entries = jax.random.normal(stream_key, extent, jnp.float32) * scale
    if len(cuts) > 0:
        entries = levels(stream_key, extent, cuts, -0.22, 0.18) * entries
    return jnp.clip(entries, min=-limit, max=limit).astype(kind)


def setup_inputs(seed: int = 0, part: int = 0) -> dict:
    key_of = jax.random.split(jax.random.key(seed), 17)
    part_splits = jax.random.split(jax.random.fold_in(key_of[16], part), 17)
    return {
        "features": bell_draw(part_splits[0], (NODES, D), 1.0, 6.0, ((0, 16),)),
        "tiles": bell_draw(part_splits[1], (SLOTS, TILE, TILE), (TILE * MAXB // 6) ** -0.5, 0.1875, ((0, 16),)),
        "block_rows": draw_block_rows(jax.random.fold_in(jax.random.fold_in(key_of[16], part), 71), part),
        "block_cols": draw_block_cols(jax.random.fold_in(jax.random.fold_in(key_of[16], part), 71), part),
        "block_count": draw_block_count(jax.random.fold_in(jax.random.fold_in(key_of[16], part), 71), part),
        "ln_gain": jnp.clip(1.0 + 0.18 * jax.random.normal(key_of[5], (D,), jnp.float32), 0.1, 1.9),
        "w_msg": bell_draw(key_of[6], (D, D), D ** -0.5, 0.25),
        "w_query": bell_draw(key_of[7], (D, D), D ** -0.5, 0.25),
        "w_key": bell_draw(key_of[8], (D, D), D ** -0.5, 0.25),
        "w_value": bell_draw(key_of[9], (D, D), D ** -0.5, 0.25),
        "w_gate": bell_draw(key_of[10], (D, D), D ** -0.5, 0.25),
        "w_out": bell_draw(key_of[11], (D, D), D ** -0.5, 0.25),
        "omega": bell_draw(key_of[12], (HDIM, FEAT), 1.0, 4.0, (), jnp.float32),
        "ln2_gain": jnp.clip(1.0 + 0.18 * jax.random.normal(key_of[13], (D,), jnp.float32), 0.1, 1.9),
        "w_up": bell_draw(key_of[14], (D, FFN), D ** -0.5, 0.25),
        "w_down": bell_draw(key_of[15], (FFN, D), FFN ** -0.5, 0.1875),
    }


def layer_norm(values, gain):
    mean = lax.optimization_barrier(jnp.mean(values, axis=-1, keepdims=True))
    centered = values - mean
    var = lax.optimization_barrier(jnp.mean(centered * centered, axis=-1, keepdims=True))
    return centered * lax.rsqrt(var + 1e-05) * gain

def device_messages(tiles_dev, rows_dev, cols_dev, count_dev, message_src):
    blocks = message_src.reshape(NCB, TILE, D)[cols_dev]
    prod = jnp.einsum('sij,sjd->sid', tiles_dev.astype(jnp.float32), blocks.astype(jnp.float32), precision=lax.Precision.HIGHEST)
    valid = (jnp.arange(MAXB, dtype=jnp.int32) < count_dev).astype(jnp.float32)
    onehot = (rows_dev[:, None] == jnp.arange(RB, dtype=jnp.int32)[None, :]).astype(jnp.float32) * valid[:, None]
    local = jnp.einsum('sr,sid->rid', onehot, prod, precision=lax.Precision.HIGHEST)
    return local.reshape(NODE_DEV, D)

def reference(features, tiles, block_rows, block_cols, block_count, ln_gain, w_msg, w_query, w_key, w_value, w_gate, w_out, omega, ln2_gain, w_up, w_down):
    hp = lax.Precision.HIGHEST
    base = features.astype(jnp.float32)
    normed = layer_norm(base, ln_gain).astype(jnp.bfloat16)
    message_src = jnp.dot(normed, w_msg, preferred_element_type=jnp.float32).astype(jnp.bfloat16)
    per_dev = lax.map(lambda item: device_messages(item[0], item[1], item[2], item[3], message_src), (tiles.reshape(N_BLK, MAXB, TILE, TILE), block_rows.reshape(N_BLK, MAXB), block_cols.reshape(N_BLK, MAXB), block_count))
    local = per_dev.reshape(NODES, D)
    scale = HDIM ** (-0.25)
    query = jnp.dot(normed, w_query, preferred_element_type=jnp.float32).reshape(NODES, HEADS, HDIM) * scale
    keys = jnp.dot(normed, w_key, preferred_element_type=jnp.float32).reshape(NODES, HEADS, HDIM) * scale
    values = jnp.dot(normed, w_value, preferred_element_type=jnp.float32).reshape(NODES, HEADS, HDIM)
    qfeat = jnp.exp(jnp.einsum('nhe,em->nhm', query, omega, precision=hp))
    kfeat = jnp.exp(jnp.einsum('nhe,em->nhm', keys, omega, precision=hp) - 0.5 * lax.optimization_barrier(jnp.sum(keys * keys, axis=-1, keepdims=True)))
    kvsum = jnp.einsum('nhm,nhe->hme', kfeat, values, precision=hp)
    ksum = lax.optimization_barrier(jnp.sum(kfeat, axis=0))
    numer = jnp.einsum('nhm,hme->nhe', qfeat, kvsum, precision=hp)
    denom = jnp.einsum('nhm,hm->nh', qfeat, ksum, precision=hp)
    attn = (numer / denom[:, :, None]).reshape(NODES, D)
    gate = jax.nn.sigmoid(jnp.dot(normed, w_gate, preferred_element_type=jnp.float32))
    gated = (attn * gate).astype(jnp.bfloat16)
    mixed = base + local + jnp.dot(gated, w_out, preferred_element_type=jnp.float32)
    second = layer_norm(mixed, ln2_gain).astype(jnp.bfloat16)
    inner = jax.nn.relu(jnp.dot(second, w_up, preferred_element_type=jnp.float32)).astype(jnp.bfloat16)
    return (mixed + jnp.dot(inner, w_down, preferred_element_type=jnp.float32)).astype(jnp.bfloat16)
```

```python
import jax
import jax.numpy as jnp
from jax import lax
from jax.experimental import pallas as pl
from jax.experimental.pallas import tpu as pltpu
from jax.sharding import PartitionSpec as P

HEADS = 8
EPS = 1e-05
F32 = jnp.float32
BF16 = jnp.bfloat16
VMEM = pl.BlockSpec(memory_space=pltpu.VMEM)
SMEM = pl.BlockSpec(memory_space=pltpu.SMEM)


def dot(a, b):
    return jnp.dot(a, b, preferred_element_type=F32)


def split(value):
    high = value.astype(BF16)
    return high, (value - high.astype(F32)).astype(BF16)


def layer_norm(values, gain):
    mean = jnp.mean(values, axis=-1, keepdims=True)
    centered = values - mean
    var = jnp.mean(centered * centered, axis=-1, keepdims=True)
    return (centered * lax.rsqrt(var + EPS) * gain).astype(BF16)


def call(body, outs, specs, args, flops, nbytes):
    return pl.pallas_call(
        body,
        out_shape=outs,
        in_specs=specs,
        out_specs=jax.tree.map(lambda _: VMEM, outs),
        compiler_params=pltpu.CompilerParams(vmem_limit_bytes=56 * 1024 * 1024),
        cost_estimate=pl.CostEstimate(flops=flops, bytes_accessed=nbytes, transcendentals=0),
    )(*args)


def sds(shape, dtype):
    return jax.ShapeDtypeStruct(shape, dtype)


def pair_ones(rows, lanes):
    top = lax.broadcasted_iota(jnp.int32, (rows, lanes), 0) < rows // 2
    left = lax.broadcasted_iota(jnp.int32, (rows, lanes), 1) < lanes // 2
    return jnp.where(top == left, 1.0, 0.0)


def pair_omega(omega):
    zero = jnp.zeros_like(omega)
    return jnp.concatenate(
        [jnp.concatenate([omega, zero], axis=1), jnp.concatenate([zero, omega], axis=1)], axis=0
    )


def message_kernel(x_ref, gain_ref, w_ref, normed_ref, msg_ref):
    normed = layer_norm(x_ref[...].astype(F32), gain_ref[...])
    normed_ref[...] = normed
    msg_ref[...] = dot(normed, w_ref[...]).astype(BF16)


def kv_kernel(core_ref, normed_ref, wk_ref, wv_ref, omega_ref, mine_ref, other_ref):
    normed = normed_ref[...]
    width = normed.shape[1]
    head = width // HEADS
    feat = omega_ref.shape[1]
    keys = dot(normed, wk_ref[...]) * (head ** (-0.25))
    values = dot(normed, wv_ref[...])
    high, low = split(pair_omega(omega_ref[...]))
    ones = (-0.5 * pair_ones(2 * head, 2 * feat)).astype(BF16)
    first = jnp.concatenate([high, high], axis=0)
    second = jnp.concatenate([low, ones, ones], axis=0)
    left = lax.broadcasted_iota(jnp.int32, (feat, 2 * head), 1) < head
    blocks, sums = [], []
    for pair in range(HEADS // 2):
        cols = slice(pair * 2 * head, (pair + 1) * 2 * head)
        k_pair = keys[:, cols]
        k_high, k_low = split(k_pair)
        s_high, s_low = split(k_pair * k_pair)
        logits = dot(jnp.concatenate([k_high, k_low], axis=1), first) + dot(
            jnp.concatenate([k_high, s_high, s_low], axis=1), second
        )
        kfeat = jnp.exp(logits)
        total = jnp.sum(kfeat, axis=0, keepdims=True)
        sums += [total[:, :feat], total[:, feat:]]
        f_high, f_low = split(kfeat)
        v_high, v_low = split(values[:, cols])
        dims = (((0,), (0,)), ((), ()))
        product = lax.dot_general(f_high, v_high, dims, preferred_element_type=F32)
        product += lax.dot_general(f_low, v_high, dims, preferred_element_type=F32)
        product += lax.dot_general(f_high, v_low, dims, preferred_element_type=F32)
        blocks.append(jnp.where(left, product[:feat], product[feat:]))
    half = HEADS // 4
    pad = jnp.zeros((16 - 2 * half, feat), F32)
    low_part = jnp.concatenate(blocks[:half] + sums[: 2 * half] + [pad], axis=0)
    high_part = jnp.concatenate(blocks[half:] + sums[2 * half :] + [pad], axis=0)
    first_core = core_ref[0] == 0
    mine_ref[...] = jnp.where(first_core, low_part, high_part)
    other_ref[...] = jnp.where(first_core, high_part, low_part).astype(BF16)


def query_kernel(normed_ref, wq_ref, wg_ref, omega_ref, qf_ref, gate_ref):
    normed = normed_ref[...]
    width = normed.shape[1]
    head = width // HEADS
    feat = omega_ref.shape[1]
    query = dot(normed, wq_ref[...]) * (head ** (-0.25))
    high, low = split(pair_omega(omega_ref[...]))
    first = jnp.concatenate([high, high], axis=0)
    for pair in range(HEADS // 2):
        q_high, q_low = split(query[:, pair * 2 * head : (pair + 1) * 2 * head])
        logits = dot(jnp.concatenate([q_high, q_low], axis=1), first) + dot(q_high, low)
        qf_ref[:, pair * 2 * feat : (pair + 1) * 2 * feat] = jnp.exp(logits).astype(BF16)
    gate_ref[...] = jax.nn.sigmoid(dot(normed, wg_ref[...]))


def place_kernel(rows_ref, cols_ref, count_ref, tiles_ref, dense_ref):
    dense_ref[...] = jnp.zeros_like(dense_ref)

    def body(slot, carry):
        dense_ref[cols_ref[slot], rows_ref[slot]] = tiles_ref[slot]
        return carry

    lax.fori_loop(0, count_ref[0], body, 0)


def attend_kernel(core_ref, x_ref, qf_ref, gate_ref, own_ref, swapped_ref, wo_ref, mixed_ref):
    feat = own_ref.shape[1]
    width = x_ref.shape[1]
    head = width // HEADS
    half = HEADS // 4
    own = own_ref[...]
    swapped = swapped_ref[...].astype(F32)
    first_core = core_ref[0] == 0
    parts = [jnp.where(first_core, own, swapped), jnp.where(first_core, swapped, own)]
    left = lax.broadcasted_iota(jnp.int32, (feat, 2 * head), 1) < head
    ones = pair_ones(2 * feat, 2 * head).astype(BF16)
    joined = []
    for pair in range(HEADS // 2):
        part = parts[pair // half]
        place = pair % half
        block = part[place * feat : (place + 1) * feat]
        block = jnp.concatenate([jnp.where(left, block, 0.0), jnp.where(left, 0.0, block)], axis=0)
        base = half * feat + 2 * place
        ksum = jnp.concatenate([part[base : base + 1], part[base + 1 : base + 2]], axis=1)
        q_pair = qf_ref[:, pair * 2 * feat : (pair + 1) * 2 * feat]
        numer = dot(q_pair, block.astype(BF16))
        d_high, d_low = split(q_pair.astype(F32) * ksum)
        denom = dot(d_high, ones) + dot(d_low, ones)
        joined.append(numer / denom)
    attn = jnp.concatenate(joined, axis=1)
    gated = (attn * gate_ref[...]).astype(BF16)
    mixed_ref[...] = x_ref[...].astype(F32) + dot(gated, wo_ref[...])


def add_messages(total, dense_ref, source_ref, start, chunks):
    for place, chunk in enumerate(chunks):
        device = source_ref[start + place]
        tile = dense_ref.shape[2]
        rows = dense_ref.shape[1]
        per = chunk.shape[0] // tile
        weights = jnp.concatenate(
            [
                jnp.concatenate([dense_ref[device * per + col, row] for col in range(per)], axis=1)
                for row in range(rows)
            ],
            axis=0,
        )
        total = total + dot(weights, chunk[...])
    return total


def early_kernel(source_ref, mixed_ref, dense_ref, *refs):
    refs[-1][...] = add_messages(mixed_ref[...], dense_ref, source_ref, 0, refs[:-1])


def solution(mesh):
    size = mesh.shape["blk"]
    chips = size // 2
    order = chip_order(mesh, size)

    def step(value, shift):
        pairs = [
            (order[p] * 2 + c, order[(p + shift) % chips] * 2 + c)
            for p in range(chips)
            for c in range(2)
        ]
        return lax.ppermute(value, "blk", pairs)

    def flip(value, bit):
        return lax.ppermute(value, "blk", [(i, i ^ bit) for i in range(size)])

    def on_device(
        features,
        tiles,
        block_rows,
        block_cols,
        block_count,
        ln_gain,
        w_msg,
        w_query,
        w_key,
        w_value,
        w_gate,
        w_out,
        omega,
        ln2_gain,
        w_up,
        w_down,
    ):
        nodes, width = features.shape
        tile = tiles.shape[1]
        feat = omega.shape[1]
        head = width // HEADS
        row_blocks = nodes // tile
        me = lax.axis_index("blk")
        core = (me % 2).reshape(1)
        normed, message = call(
            message_kernel,
            (sds((nodes, width), BF16), sds((nodes, width), BF16)),
            [VMEM] * 3,
            (features, ln_gain.reshape(1, width), w_msg),
            2 * nodes * width * width,
            2 * (width * width + 3 * nodes * width),
        )

        stages = [[message, flip(message, 1)]]
        sources = [[0, 0]]
        ahead = back = message
        full = (chips - 1) // 2
        for k in range(1, full + 1):
            ahead = step(ahead, 1)
            back = step(back, -1)
            stages.append([ahead, back, flip(ahead, 1), flip(back, 1)])
            sources.append([k, -k, k, -k])
        if chips % 2 == 0:
            half = nodes // 2
            upper = step(ahead[:half], 1)
            lower = step(back[half:], -1)
            last = jnp.concatenate([upper, lower], axis=0)
            stages.append([last, flip(last, 1)])
            sources.append([chips // 2] * 2)
        place = {chip: p for p, chip in enumerate(order)}
        table = []
        for device in range(size):
            entries = []
            for stage in sources:
                for i, shift in enumerate(stage):
                    chip = order[(place[device // 2] - shift) % chips]
                    same = i < len(stage) // 2
                    entries.append(chip * 2 + (device % 2 if same else 1 - device % 2))
            table.append(entries)
        source = jnp.asarray(table, jnp.int32)[me]

        rows = HEADS // 4 * feat + 16
        own, other = call(
            kv_kernel,
            (sds((rows, feat), F32), sds((rows, feat), BF16)),
            [SMEM] + [VMEM] * 4,
            (core, normed, w_key, w_value, omega),
            6 * nodes * width * width,
            4 * width * width,
        )
        own = own + flip(other, 1).astype(F32)
        if chips & (chips - 1) == 0:
            bit = 2
            while bit < size:
                own = own + flip(own.astype(BF16), bit).astype(F32)
                bit *= 2
        else:
            own = lax.psum(
                own, "blk", axis_index_groups=[list(range(c, size, 2)) for c in range(2)]
            )
        swapped = flip(own.astype(BF16), 1)

        qfeat, gate = call(
            query_kernel,
            (sds((nodes, HEADS * feat), BF16), sds((nodes, width), F32)),
            [VMEM] * 4,
            (normed, w_query, w_gate, omega),
            6 * nodes * width * width,
            4 * width * width,
        )
        dense = call(
            place_kernel,
            sds((size * row_blocks, row_blocks, tile, tile), BF16),
            [SMEM] * 3 + [VMEM],
            (block_rows, block_cols, block_count, tiles),
            0,
            4 * tiles.size,
        )
        mixed = call(
            attend_kernel,
            sds((nodes, width), F32),
            [SMEM] + [VMEM] * 6,
            (core, features, qfeat, gate, own, swapped, w_out),
            4 * nodes * width * width,
            4 * width * width,
        )
        early = [chunk for stage in stages[:-1] for chunk in stage]
        late = stages[-1]
        mixed = call(
            early_kernel,
            sds((nodes, width), F32),
            [SMEM] + [VMEM] * (2 + len(early)),
            (source, mixed, dense, *early),
            2 * nodes * nodes * width * len(early),
            2 * nodes * width * len(early),
        )
        start = len(early)

        def final_kernel(source_ref, mixed_ref, dense_ref, gain_ref, up_ref, down_ref, *refs):
            mixed = add_messages(mixed_ref[...], dense_ref, source_ref, start, refs[:-1])
            second = layer_norm(mixed, gain_ref[...])
            inner = jnp.maximum(dot(second, up_ref[...]), 0.0).astype(BF16)
            refs[-1][...] = (mixed + dot(inner, down_ref[...])).astype(BF16)

        return call(
            final_kernel,
            sds((nodes, width), BF16),
            [SMEM] + [VMEM] * (5 + len(late)),
            (source, mixed, dense, ln2_gain.reshape(1, width), w_up, w_down, *late),
            4 * nodes * width * w_up.shape[1],
            4 * width * w_up.shape[1],
        )

    split_rows = P(("groups", "blk"))
    return jax.shard_map(
        on_device,
        mesh=mesh,
        in_specs=(split_rows,) * 5 + (P(),) * 11,
        out_specs=P(("groups", "blk"), None),
        check_vma=False,
    )


def chip_order(mesh, size):
    devices = mesh.devices.reshape(-1, size)[0]
    coords = [getattr(d, "coords", None) for d in devices[::2]]
    if any(c is None for c in coords) or len({c[1] for c in map(tuple, coords)}) != 2:
        return list(range(size // 2))
    low = min(c[1] for c in coords)
    up = sorted((i for i, c in enumerate(coords) if c[1] == low), key=lambda i: coords[i][2])
    down = sorted((i for i, c in enumerate(coords) if c[1] != low), key=lambda i: -coords[i][2])
    return up + down
```

```python
import jax
import jax.numpy as jnp
from jax import lax
from jax.experimental import pallas as pl
from jax.experimental.pallas import tpu as pltpu
from jax.sharding import PartitionSpec as P

HEADS = 8
EPS = 1e-05
F32 = jnp.float32
BF16 = jnp.bfloat16
VMEM = pl.BlockSpec(memory_space=pltpu.VMEM)
SMEM = pl.BlockSpec(memory_space=pltpu.SMEM)
HBM = pl.BlockSpec(memory_space=pltpu.HBM)


def dot(a, b):
    return jnp.dot(a, b, preferred_element_type=F32)


def split(value):
    high = value.astype(BF16)
    return high, (value - high.astype(F32)).astype(BF16)


def layer_norm(values, gain):
    mean = jnp.mean(values, axis=-1, keepdims=True)
    centered = values - mean
    var = jnp.mean(centered * centered, axis=-1, keepdims=True)
    return (centered * lax.rsqrt(var + EPS) * gain).astype(BF16)


def call(body, outs, specs, args, scratch=(), limit=None):
    held = sum(a.size * a.dtype.itemsize for a in (*args, *jax.tree.leaves(outs)))
    limit = limit or held // 2**20 + 7
    return pl.pallas_call(
        body,
        out_shape=outs,
        in_specs=specs,
        out_specs=jax.tree.map(lambda _: VMEM, outs),
        scratch_shapes=scratch,
        compiler_params=pltpu.CompilerParams(vmem_limit_bytes=limit * 2**20),
        cost_estimate=pl.CostEstimate(flops=1, bytes_accessed=1, transcendentals=0),
    )(*args)


def after(values, *others):
    any_space = pl.BlockSpec(memory_space=pl.ANY)
    return pl.pallas_call(
        lambda *refs: None,
        out_shape=[sds(v.shape, v.dtype) for v in values],
        in_specs=[any_space] * (len(values) + len(others)),
        out_specs=[any_space] * len(values),
        input_output_aliases={i: i for i in range(len(values))},
        compiler_params=pltpu.CompilerParams(vmem_limit_bytes=2**20),
        cost_estimate=pl.CostEstimate(flops=1, bytes_accessed=1, transcendentals=0),
    )(*values, *others)


def sds(shape, dtype):
    return jax.ShapeDtypeStruct(shape, dtype)


def pair_ones(rows, lanes):
    top = lax.broadcasted_iota(jnp.int32, (rows, lanes), 0) < rows // 2
    left = lax.broadcasted_iota(jnp.int32, (rows, lanes), 1) < lanes // 2
    return jnp.where(top == left, 1.0, 0.0)


def pair_omega(omega):
    zero = jnp.zeros_like(omega)
    return jnp.concatenate(
        [jnp.concatenate([omega, zero], axis=1), jnp.concatenate([zero, omega], axis=1)], axis=0
    )


class Fetch:
    def __init__(self, source, target, sems, pieces):
        rows = source.shape[0] // pieces
        self.copies = [
            pltpu.make_async_copy(
                source.at[pl.ds(i * rows, rows)], target.at[pl.ds(i * rows, rows)], sems.at[i]
            )
            for i in range(pieces)
        ]
        for copy in self.copies:
            copy.start()

    def wait(self):
        for copy in self.copies:
            copy.wait()


def buffers(*fetches):
    return [pltpu.VMEM(a.shape, a.dtype) for a, _ in fetches] + [
        pltpu.SemaphoreType.DMA((pieces,)) for _, pieces in fetches
    ]


PIECES = 4
EXTRA = 56


def message_kernel(
    core_ref,
    x_hbm,
    sibling_hbm,
    gain_hbm,
    w_hbm,
    normed_ref,
    msg_ref,
    x_ref,
    sibling_ref,
    gain_ref,
    w_ref,
    x_sem,
    sibling_sem,
    gain_sem,
    w_sem,
):
    nodes, width = x_hbm.shape
    core = core_ref[0]
    half = pl.ds(pl.multiple_of(core * (width // 2), width // 2), width // 2)
    x_copy = Fetch(x_hbm, x_ref, x_sem, PIECES)
    sibling_copy = Fetch(sibling_hbm, sibling_ref, sibling_sem, PIECES)
    gain_copy = Fetch(gain_hbm, gain_ref, gain_sem, 1)
    w_copy = Fetch(w_hbm.at[:, half], w_ref, w_sem, PIECES)
    gain_copy.wait()
    gain = gain_ref[...]
    mine = pl.ds(pl.multiple_of(core * nodes, nodes), nodes)
    theirs = pl.ds(pl.multiple_of((1 - core) * nodes, nodes), nodes)
    x_copy.wait()
    normed = layer_norm(x_ref[...].astype(F32), gain)
    normed_ref[mine, :] = normed
    w_copy.wait()
    msg_ref[mine, :] = dot(normed, w_ref[...]).astype(BF16)
    sibling_copy.wait()
    normed = layer_norm(sibling_ref[...].astype(F32), gain)
    normed_ref[theirs, :] = normed
    msg_ref[theirs, :] = dot(normed, w_ref[...]).astype(BF16)


def kv_kernel(core_ref, normed_ref, wk_ref, wv_ref, omega_ref, sums_ref):
    width = normed_ref.shape[1]
    head = width // HEADS
    feat = omega_ref.shape[1]
    half = HEADS // 4
    cols = pl.ds(pl.multiple_of(core_ref[0] * (width // 2), width // 2), width // 2)
    normed = normed_ref[...]
    keys = dot(normed, wk_ref[:, cols]) * (head ** (-0.25))
    values = dot(normed, wv_ref[:, cols])
    high, low = split(pair_omega(omega_ref[...]))
    ones = (-0.5 * pair_ones(2 * head, 2 * feat)).astype(BF16)
    first = jnp.concatenate([high, high], axis=0)
    second = jnp.concatenate([low, ones, ones], axis=0)
    left = lax.broadcasted_iota(jnp.int32, (feat, 2 * head), 1) < head
    for pair in range(half):
        k_pair = keys[:, pair * 2 * head : (pair + 1) * 2 * head]
        k_high, k_low = split(k_pair)
        s_high, s_low = split(k_pair * k_pair)
        logits = dot(jnp.concatenate([k_high, k_low], axis=1), first) + dot(
            jnp.concatenate([k_high, s_high, s_low], axis=1), second
        )
        kfeat = jnp.exp(logits)
        total = jnp.sum(kfeat, axis=0, keepdims=True)
        base = half * feat + 2 * pair
        sums_ref[base : base + 1, :] = total[:, :feat]
        sums_ref[base + 1 : base + 2, :] = total[:, feat:]
        f_high, f_low = split(kfeat)
        v_high, v_low = split(values[:, pair * 2 * head : (pair + 1) * 2 * head])
        dims = (((0,), (0,)), ((), ()))
        product = lax.dot_general(f_high, v_high, dims, preferred_element_type=F32)
        product += lax.dot_general(f_low, v_high, dims, preferred_element_type=F32)
        product += lax.dot_general(f_high, v_low, dims, preferred_element_type=F32)
        sums_ref[pair * feat : (pair + 1) * feat, :] = jnp.where(
            left, product[:feat], product[feat:]
        )
    used = half * feat + 2 * half
    sums_ref[used:, :] = jnp.zeros((sums_ref.shape[0] - used, feat), F32)


def query_kernel(core_ref, normed_ref, wq_ref, wg_ref, omega_ref, qf_ref, gate_ref):
    nodes = qf_ref.shape[0]
    normed = normed_ref[pl.ds(pl.multiple_of(core_ref[0] * nodes, nodes), nodes), :]
    width = normed.shape[1]
    head = width // HEADS
    feat = omega_ref.shape[1]
    query = dot(normed, wq_ref[...]) * (head ** (-0.25))
    high, low = split(pair_omega(omega_ref[...]))
    first = jnp.concatenate([high, high], axis=0)
    for pair in range(HEADS // 2):
        q_high, q_low = split(query[:, pair * 2 * head : (pair + 1) * 2 * head])
        logits = dot(jnp.concatenate([q_high, q_low], axis=1), first) + dot(q_high, low)
        qf_ref[:, pair * 2 * feat : (pair + 1) * 2 * feat] = jnp.exp(logits).astype(BF16)
    gate_ref[...] = jax.nn.sigmoid(dot(normed, wg_ref[...]))


def place_kernel(rows_ref, cols_ref, count_ref, tiles_ref, before_ref, dense_ref):
    del before_ref
    dense_ref[...] = jnp.zeros_like(dense_ref)

    def body(slot, carry):
        dense_ref[cols_ref[slot], rows_ref[slot]] = tiles_ref[slot]
        return carry

    lax.fori_loop(0, count_ref[0], body, 0)


def attend_kernel(core_ref, x_ref, qf_ref, gate_ref, own_ref, swapped_ref, wo_ref, mixed_ref):
    feat = own_ref.shape[1]
    width = x_ref.shape[1]
    head = width // HEADS
    half = HEADS // 4
    own = own_ref[...]
    swapped = swapped_ref[...].astype(F32)
    first_core = core_ref[0] == 0
    parts = [jnp.where(first_core, own, swapped), jnp.where(first_core, swapped, own)]
    left = lax.broadcasted_iota(jnp.int32, (feat, 2 * head), 1) < head
    ones = pair_ones(2 * feat, 2 * head).astype(BF16)
    joined = []
    for pair in range(HEADS // 2):
        part = parts[pair // half]
        place = pair % half
        block = part[place * feat : (place + 1) * feat]
        block = jnp.concatenate([jnp.where(left, block, 0.0), jnp.where(left, 0.0, block)], axis=0)
        base = half * feat + 2 * place
        ksum = jnp.concatenate([part[base : base + 1], part[base + 1 : base + 2]], axis=1)
        q_pair = qf_ref[:, pair * 2 * feat : (pair + 1) * 2 * feat]
        numer = dot(q_pair, block.astype(BF16))
        d_high, d_low = split(q_pair.astype(F32) * ksum)
        denom = dot(d_high, ones) + dot(d_low, ones)
        joined.append(numer / denom)
    attn = jnp.concatenate(joined, axis=1)
    gated = (attn * gate_ref[...]).astype(BF16)
    mixed_ref[...] = x_ref[...].astype(F32) + dot(gated, wo_ref[...])


def product(dense_ref, column, chunk):
    rows, tile = dense_ref.shape[1:3]
    weights = [
        jnp.concatenate(
            [dense_ref[column + col, row] for col in range(chunk.shape[0] // tile)], axis=1
        )
        for row in range(rows)
    ]
    return dot(jnp.concatenate(weights, axis=0), chunk)


def solution(mesh):
    size = mesh.shape["blk"]
    chips = size // 2
    order = chip_order(mesh, size)

    def step(value, shift):
        pairs = [
            (order[p] * 2 + c, order[(p + shift) % chips] * 2 + c)
            for p in range(chips)
            for c in range(2)
        ]
        return lax.ppermute(value, "blk", pairs)

    def flip(value, bit):
        return lax.ppermute(value, "blk", [(i, i ^ bit) for i in range(size)])

    def on_device(
        features,
        tiles,
        block_rows,
        block_cols,
        block_count,
        ln_gain,
        w_msg,
        w_query,
        w_key,
        w_value,
        w_gate,
        w_out,
        omega,
        ln2_gain,
        w_up,
        w_down,
    ):
        nodes, width = features.shape
        tile = tiles.shape[1]
        feat = omega.shape[1]
        head = width // HEADS
        row_blocks = nodes // tile
        me = lax.axis_index("blk")
        core = (me % 2).reshape(1)
        half = width // 2
        normed, message = call(
            message_kernel,
            (sds((2 * nodes, width), BF16), sds((2 * nodes, half), BF16)),
            [SMEM] + [HBM] * 4,
            (core, features, flip(features, 1), ln_gain.reshape(1, width), w_msg),
            buffers(
                (features, PIECES),
                (features, PIECES),
                (sds((1, width), F32), 1),
                (sds((width, half), BF16), PIECES),
            ),
            EXTRA,
        )

        first_ahead, first_back = step(message, 1), step(message, -1)

        rows = HEADS // 4 * feat + 16
        own = call(
            kv_kernel,
            sds((rows, feat), F32),
            [SMEM] + [VMEM] * 4,
            (core, normed, w_key, w_value, omega),
        )
        first_ahead, first_back = after([first_ahead, first_back], own)
        if chips & (chips - 1) == 0:
            bit = size // 2
            while bit > 1:
                own = own + flip(own.astype(BF16), bit).astype(F32)
                bit //= 2
        else:
            own = lax.psum(
                own, "blk", axis_index_groups=[list(range(c, size, 2)) for c in range(2)]
            )
        swapped = flip(own.astype(BF16), 1)

        qfeat, gate = call(
            query_kernel,
            (sds((nodes, HEADS * feat), BF16), sds((nodes, width), F32)),
            [SMEM] + [VMEM] * 4,
            (core, normed, w_query, w_gate, omega),
        )
        dense = call(
            place_kernel,
            sds((size * row_blocks, row_blocks, tile, tile), BF16),
            [SMEM] * 3 + [VMEM, pl.BlockSpec(memory_space=pl.ANY)],
            (block_rows, block_cols, block_count, tiles, first_ahead),
        )
        sibling = flip(dense, 1)
        mixed = call(
            attend_kernel,
            sds((nodes, width), F32),
            [SMEM] + [VMEM] * 6,
            (core, features, qfeat, gate, own, swapped, w_out),
        )

        full = (chips - 1) // 2
        shifts = [0] + [sign * k for k in range(1, full + 1) for sign in (1, -1)]
        if chips % 2 == 0:
            shifts += [chips // 2]
        home = {chip: p for p, chip in enumerate(order)}
        table = jnp.asarray(
            [order[(home[chip] - shift) % chips] for chip in range(chips) for shift in shifts],
            jnp.int32,
        )

        def accumulate(totals, first, chunks):
            totals = list(totals)

            def body(me_ref, table_ref, mine_ref, sibling_ref, *refs):
                outs = refs[-2:]
                chunk_refs = refs[len(totals) : -2]
                for dense_ref, total, out in zip((mine_ref, sibling_ref), refs, outs):
                    value = total[...] if totals else None
                    place, rows_seen = first, 0
                    for chunk_ref in chunk_refs:
                        chip = table_ref[(me_ref[0] // 2) * chips + place]
                        column = chip * (2 * nodes // tile) + rows_seen // tile
                        part = product(dense_ref, column, chunk_ref[...])
                        value = part if value is None else value + part
                        rows_seen += chunk_ref.shape[0]
                        if rows_seen == 2 * nodes:
                            place, rows_seen = place + 1, 0
                    out[...] = value

            return call(
                body,
                (sds((nodes, half), F32), sds((nodes, half), F32)),
                [SMEM] * 2 + [VMEM] * (2 + len(totals) + len(chunks)),
                (me.reshape(1), table, dense, sibling, *totals, *chunks),
            )

        ahead, back = first_ahead, first_back
        chunks = [message, ahead, back]
        totals, used = (), 0
        for k in range(2, full + 1):
            if k == 3:
                ahead, back = after([ahead, back], qfeat, dense)
                chunks[-2:] = [ahead, back]
            if k > 3:
                ready = 1 + 2 * (k - 2)
                totals = accumulate(totals, used, chunks[used:ready])
                used = ready
            ahead, back = step(ahead, 1), step(back, -1)
            chunks += [ahead, back]
        ready = 1 + 2 * (full - 1)
        totals = accumulate(totals, used, chunks[used:ready])
        used = ready
        ahead, back = after([ahead, back], totals[0])
        chunks[-2:] = [ahead, back]
        late = []
        if chips % 2 == 0:
            late = [step(ahead[:nodes], 1), step(back[nodes:], -1)]
            totals = accumulate(totals, used, chunks[used:])
            used = len(chunks)
        totals = accumulate(totals, used, late or chunks[used:])
        theirs = flip(totals[1], 1)

        def final_kernel(core_ref, mixed_ref, mine_ref, theirs_ref, gain_ref, up_ref, down_ref, out_ref):
            first_core = core_ref[0] == 0
            mine, theirs = mine_ref[...], theirs_ref[...]
            local = jnp.concatenate(
                [jnp.where(first_core, mine, theirs), jnp.where(first_core, theirs, mine)], axis=1
            )
            mixed = mixed_ref[...] + local
            second = layer_norm(mixed, gain_ref[...])
            inner = jnp.maximum(dot(second, up_ref[...]), 0.0).astype(BF16)
            out_ref[...] = (mixed + dot(inner, down_ref[...])).astype(BF16)

        return call(
            final_kernel,
            sds((nodes, width), BF16),
            [SMEM] + [VMEM] * 6,
            (core, mixed, totals[0], theirs, ln2_gain.reshape(1, width), w_up, w_down),
        )

    split_rows = P(("groups", "blk"))
    return jax.shard_map(
        on_device,
        mesh=mesh,
        in_specs=(split_rows,) * 5 + (P(),) * 11,
        out_specs=P(("groups", "blk"), None),
        check_vma=False,
    )


def chip_order(mesh, size):
    devices = mesh.devices.reshape(-1, size)[0]
    coords = [getattr(d, "coords", None) for d in devices[::2]]
    if any(c is None for c in coords) or len({c[1] for c in map(tuple, coords)}) != 2:
        return list(range(size // 2))
    low = min(c[1] for c in coords)
    up = sorted((i for i, c in enumerate(coords) if c[1] == low), key=lambda i: coords[i][2])
    down = sorted((i for i, c in enumerate(coords) if c[1] != low), key=lambda i: -coords[i][2])
    return up + down
```

```python
import jax
import jax.numpy as jnp
from jax import lax
from jax.experimental import pallas as pl
from jax.experimental.pallas import tpu as pltpu
from jax.sharding import PartitionSpec as P

HEADS = 8
EPS = 1e-05
F32 = jnp.float32
BF16 = jnp.bfloat16
VMEM = pl.BlockSpec(memory_space=pltpu.VMEM)
SMEM = pl.BlockSpec(memory_space=pltpu.SMEM)
HBM = pl.BlockSpec(memory_space=pltpu.HBM)


def dot(a, b):
    return jnp.dot(a, b, preferred_element_type=F32)


def split(value):
    high = value.astype(BF16)
    return high, (value - high.astype(F32)).astype(BF16)


def layer_norm(values, gain):
    mean = jnp.mean(values, axis=-1, keepdims=True)
    centered = values - mean
    var = jnp.mean(centered * centered, axis=-1, keepdims=True)
    return (centered * lax.rsqrt(var + EPS) * gain).astype(BF16)


def call(body, outs, specs, args, scratch=(), limit=None):
    held = sum(a.size * a.dtype.itemsize for a in (*args, *jax.tree.leaves(outs)))
    limit = limit or held // 2**20 + 7
    return pl.pallas_call(
        body,
        out_shape=outs,
        in_specs=specs,
        out_specs=jax.tree.map(lambda _: VMEM, outs),
        scratch_shapes=scratch,
        compiler_params=pltpu.CompilerParams(vmem_limit_bytes=int(limit * 2**20)),
        cost_estimate=pl.CostEstimate(flops=1, bytes_accessed=1, transcendentals=0),
    )(*args)


def after(values, *others):
    any_space = pl.BlockSpec(memory_space=pl.ANY)
    return pl.pallas_call(
        lambda *refs: None,
        out_shape=[sds(v.shape, v.dtype) for v in values],
        in_specs=[any_space] * (len(values) + len(others)),
        out_specs=[any_space] * len(values),
        input_output_aliases={i: i for i in range(len(values))},
        compiler_params=pltpu.CompilerParams(vmem_limit_bytes=2**20),
        cost_estimate=pl.CostEstimate(flops=1, bytes_accessed=1, transcendentals=0),
    )(*values, *others)


def sds(shape, dtype):
    return jax.ShapeDtypeStruct(shape, dtype)


def pair_ones(rows, lanes):
    top = lax.broadcasted_iota(jnp.int32, (rows, lanes), 0) < rows // 2
    left = lax.broadcasted_iota(jnp.int32, (rows, lanes), 1) < lanes // 2
    return jnp.where(top == left, 1.0, 0.0)


def pair_omega(omega):
    zero = jnp.zeros_like(omega)
    return jnp.concatenate(
        [jnp.concatenate([omega, zero], axis=1), jnp.concatenate([zero, omega], axis=1)], axis=0
    )


class Fetch:
    def __init__(self, source, target, sems, pieces):
        rows = source.shape[0] // pieces
        self.copies = [
            pltpu.make_async_copy(
                source.at[pl.ds(i * rows, rows)], target.at[pl.ds(i * rows, rows)], sems.at[i]
            )
            for i in range(pieces)
        ]
        for copy in self.copies:
            copy.start()

    def wait(self):
        for copy in self.copies:
            copy.wait()


def buffers(*fetches):
    return [pltpu.VMEM(a.shape, a.dtype) for a, _ in fetches] + [
        pltpu.SemaphoreType.DMA((pieces,)) for _, pieces in fetches
    ]


PIECES = 4
EXTRA = 56


def message_kernel(
    x_hbm, gain_hbm, w_hbm, normed_ref, msg_ref, x_ref, gain_ref, w_ref, x_sem, gain_sem, w_sem
):
    x_copy = Fetch(x_hbm, x_ref, x_sem, PIECES)
    gain_copy = Fetch(gain_hbm, gain_ref, gain_sem, 1)
    w_copy = Fetch(w_hbm, w_ref, w_sem, PIECES)
    gain_copy.wait()
    x_copy.wait()
    normed = layer_norm(x_ref[...].astype(F32), gain_ref[...])
    normed_ref[...] = normed
    w_copy.wait()
    msg_ref[...] = dot(normed, w_ref[...]).astype(BF16)


def kv_kernel(
    me_ref, normed_hbm, wk_hbm, wv_hbm, omega_hbm, own_ref, near_ref, core_ref, both_ref, sums_ref,
    normed_ref, wk_ref, wv_ref, omega_ref, normed_sem, wk_sem, wv_sem, omega_sem
):
    normed_copy = Fetch(normed_hbm, normed_ref, normed_sem, PIECES)
    wk_copy = Fetch(wk_hbm, wk_ref, wk_sem, PIECES)
    omega_copy = Fetch(omega_hbm, omega_ref, omega_sem, 1)
    wv_copy = Fetch(wv_hbm, wv_ref, wv_sem, PIECES)
    width = normed_ref.shape[1]
    head = width // HEADS
    feat = omega_ref.shape[1]
    normed_copy.wait()
    normed = normed_ref[...]
    wk_copy.wait()
    keys = dot(normed, wk_ref[...]) * (head ** (-0.25))
    omega_copy.wait()
    wv_copy.wait()
    values = dot(normed, wv_ref[...])
    high, low = split(pair_omega(omega_ref[...]))
    ones = (-0.5 * pair_ones(2 * head, 2 * feat)).astype(BF16)
    first = jnp.concatenate([high, high], axis=0)
    second = jnp.concatenate([low, ones, ones], axis=0)
    left = lax.broadcasted_iota(jnp.int32, (feat, 2 * head), 1) < head
    pad = jnp.zeros((own_ref.shape[0] - feat - 2, feat), F32)
    for pair in range(HEADS // 2):
        k_pair = keys[:, pair * 2 * head : (pair + 1) * 2 * head]
        k_high, k_low = split(k_pair)
        s_high, s_low = split(k_pair * k_pair)
        logits = dot(jnp.concatenate([k_high, k_low], axis=1), first) + dot(
            jnp.concatenate([k_high, s_high, s_low], axis=1), second
        )
        kfeat = jnp.exp(logits)
        total = jnp.sum(kfeat, axis=0, keepdims=True)
        f_high, f_low = split(kfeat)
        v_high, v_low = split(values[:, pair * 2 * head : (pair + 1) * 2 * head])
        dims = (((0,), (0,)), ((), ()))
        both = lax.dot_general(f_high, v_high, dims, preferred_element_type=F32)
        both += lax.dot_general(f_low, v_high, dims, preferred_element_type=F32)
        both += lax.dot_general(f_high, v_low, dims, preferred_element_type=F32)
        block = jnp.where(left, both[:feat], both[feat:])
        sums_ref[pair] = jnp.concatenate([block, total[:, :feat], total[:, feat:], pad], axis=0)
    mine = (me_ref[0] % 2) * 2 + (me_ref[0] // 2) % 2
    own_ref[...] = sums_ref[mine]
    near_ref[...] = sums_ref[mine ^ 1].astype(BF16)
    core_ref[...] = sums_ref[mine ^ 2].astype(BF16)
    both_ref[...] = sums_ref[mine ^ 3].astype(BF16)


def query_kernel(normed_ref, wq_ref, wg_ref, omega_ref, qf_ref, gate_ref):
    normed = normed_ref[...]
    width = normed.shape[1]
    head = width // HEADS
    feat = omega_ref.shape[1]
    query = dot(normed, wq_ref[...]) * (head ** (-0.25))
    high, low = split(pair_omega(omega_ref[...]))
    first = jnp.concatenate([high, high], axis=0)
    for pair in range(HEADS // 2):
        q_high, q_low = split(query[:, pair * 2 * head : (pair + 1) * 2 * head])
        logits = dot(jnp.concatenate([q_high, q_low], axis=1), first) + dot(q_high, low)
        qf_ref[:, pair * 2 * feat : (pair + 1) * 2 * feat] = jnp.exp(logits).astype(BF16)
    gate_ref[...] = jax.nn.sigmoid(dot(normed, wg_ref[...]))


def place_kernel(core_ref, rows_ref, cols_ref, count_ref, tiles_ref, before_ref, mine_ref, theirs_ref):
    del before_ref
    per = mine_ref.shape[1]
    mine_ref[...] = jnp.zeros_like(mine_ref)
    theirs_ref[...] = jnp.zeros_like(theirs_ref)

    def body(slot, carry):
        col, row = cols_ref[slot], rows_ref[slot]
        place = (col // (2 * per)) * per + col % per
        own = (col // per) % 2 == core_ref[0]

        @pl.when(own)
        def _():
            mine_ref[place, row] = tiles_ref[slot]

        @pl.when(jnp.logical_not(own))
        def _():
            theirs_ref[place, row] = tiles_ref[slot]

        return carry

    lax.fori_loop(0, count_ref[0], body, 0)


def attend_kernel(
    me_ref, x_ref, qf_ref, gate_ref, own_ref, pair_ref, core_ref, both_ref, wo_ref, total_ref, mixed_ref
):
    width = x_ref.shape[1]
    head = width // HEADS
    feat = own_ref.shape[1]
    mine = (me_ref[0] % 2) * 2 + (me_ref[0] // 2) % 2
    left = lax.broadcasted_iota(jnp.int32, (feat, 2 * head), 1) < head
    ones = pair_ones(2 * feat, 2 * head).astype(BF16)
    joined = []
    for pair in range(HEADS // 2):
        offset = mine ^ pair
        part = own_ref[...].astype(F32)
        for other, ref in ((1, pair_ref), (2, core_ref), (3, both_ref)):
            part = jnp.where(offset == other, ref[...].astype(F32), part)
        block = part[:feat]
        block = jnp.concatenate([jnp.where(left, block, 0.0), jnp.where(left, 0.0, block)], axis=0)
        ksum = jnp.concatenate([part[feat : feat + 1], part[feat + 1 : feat + 2]], axis=1)
        q_pair = qf_ref[:, pair * 2 * feat : (pair + 1) * 2 * feat]
        numer = dot(q_pair, block.astype(BF16))
        d_high, d_low = split(q_pair.astype(F32) * ksum)
        denom = dot(d_high, ones) + dot(d_low, ones)
        joined.append(numer / denom)
    attn = jnp.concatenate(joined, axis=1)
    gated = (attn * gate_ref[...]).astype(BF16)
    mixed_ref[...] = x_ref[...].astype(F32) + total_ref[...] + dot(gated, wo_ref[...])


def product(dense_ref, column, chunk):
    rows, tile = dense_ref.shape[1:3]
    weights = [
        jnp.concatenate(
            [dense_ref[column + col, row] for col in range(chunk.shape[0] // tile)], axis=1
        )
        for row in range(rows)
    ]
    return dot(jnp.concatenate(weights, axis=0), chunk)


def solution(mesh):
    size = mesh.shape["blk"]
    chips = size // 2
    order = chip_order(mesh, size)

    def step(value, shift):
        pairs = [
            (order[p] * 2 + c, order[(p + shift) % chips] * 2 + c)
            for p in range(chips)
            for c in range(2)
        ]
        return lax.ppermute(value, "blk", pairs)

    def flip(value, bit):
        return lax.ppermute(value, "blk", [(i, i ^ bit) for i in range(size)])

    def on_device(
        features,
        tiles,
        block_rows,
        block_cols,
        block_count,
        ln_gain,
        w_msg,
        w_query,
        w_key,
        w_value,
        w_gate,
        w_out,
        omega,
        ln2_gain,
        w_up,
        w_down,
    ):
        nodes, width = features.shape
        tile = tiles.shape[1]
        feat = omega.shape[1]
        head = width // HEADS
        row_blocks = nodes // tile
        me = lax.axis_index("blk")
        core = (me % 2).reshape(1)
        me = me.reshape(1)
        normed, message = call(
            message_kernel,
            (sds((nodes, width), BF16), sds((nodes, width), BF16)),
            [HBM] * 3,
            (features, ln_gain.reshape(1, width), w_msg),
            buffers((features, PIECES), (sds((1, width), F32), 1), (w_msg, PIECES)),
            EXTRA,
        )

        full = (chips - 1) // 2
        ahead, back = step(message, 1), step(message, -1)

        rows = feat + 16
        given = sds((rows, feat), BF16)
        own, near, across, both = call(
            kv_kernel,
            (sds((rows, feat), F32), given, given, given),
            [SMEM] + [HBM] * 4,
            (me, normed, w_key, w_value, omega),
            [pltpu.VMEM((HEADS // 2, rows, feat), F32)]
            + buffers((normed, PIECES), (w_key, PIECES), (w_value, PIECES), (omega, 1)),
            56,
        )
        ahead, back = after([ahead, back], near)
        sums = [sum((flip(v, b).astype(F32) for v, b in ((near, 2), (across, 1), (both, 3))), own)]
        bit = 4
        while bit < size:
            hops = [bit, 2 * bit, 3 * bit] if 2 * bit < size else [bit]
            sent = sums[-1].astype(BF16)
            sums.append(sum((flip(sent, hop).astype(F32) for hop in hops), sums[-1]))
            bit *= 4
        quarter = sums[-1].astype(BF16)

        qfeat, gate = call(
            query_kernel,
            (sds((nodes, HEADS * feat), BF16), sds((nodes, width), F32)),
            [VMEM] * 4,
            (normed, w_query, w_gate, omega),
        )
        blocks = sds((chips * row_blocks, row_blocks, tile, tile), BF16)
        dense, others = call(
            place_kernel,
            (blocks, blocks),
            [SMEM] * 4 + [VMEM, pl.BlockSpec(memory_space=pl.ANY)],
            (core, block_rows, block_cols, block_count, tiles, sums[0]),
        )
        shifts = [0] + [sign * k for k in range(1, full + 1) for sign in (1, -1)]
        if chips % 2 == 0:
            shifts += [chips // 2]
        home = {chip: p for p, chip in enumerate(order)}
        table = jnp.asarray(
            [order[(home[chip] - shift) % chips] for chip in range(chips) for shift in shifts],
            jnp.int32,
        )

        def accumulate(matrices, totals, first, chunks, dtype=F32):
            totals, count = list(totals), len(matrices)

            def body(me_ref, table_ref, *refs):
                for dense_ref, out, total in zip(refs, refs[-count:], totals or [None] * count):
                    value = None
                    if totals:
                        value = refs[count + [t is total for t in totals].index(True)][...]
                    place, seen = first, 0
                    for chunk_ref in refs[count + len(totals) : -count]:
                        chip = table_ref[(me_ref[0] // 2) * chips + place]
                        column = chip * row_blocks + seen // tile
                        part = product(dense_ref, column, chunk_ref[...])
                        value = part if value is None else value + part
                        seen += chunk_ref.shape[0]
                        if seen == nodes:
                            place, seen = place + 1, 0
                    out[...] = value.astype(out.dtype)

            return call(
                body,
                [sds((nodes, width), dtype)] * count,
                [SMEM] * 2 + [VMEM] * (count + len(totals) + len(chunks)),
                (me, table, *matrices, *totals, *chunks),
            )

        chunks = [message, ahead, back]
        totals, used = (), 0
        sibling = None
        for k in range(2, full + 1):
            if k == 3:
                ahead, back, others = after([ahead, back, others], dense)
                chunks[-2:] = [ahead, back]
                sibling = flip(others, 1)
            if k > 3:
                ready = 1 + 2 * (k - 2)
                totals = accumulate((dense, sibling), totals, used, chunks[used:ready])
                used = ready
                ahead, back = after([ahead, back], totals[0])
                chunks[-2:] = [ahead, back]
            ahead, back = step(ahead, 1), step(back, -1)
            chunks += [ahead, back]
        ready = 1 + 2 * (full - 1)
        totals = accumulate((dense, sibling), totals, used, chunks[used:ready])
        ahead, back = after([ahead, back], totals[0], qfeat)
        chunks[-2:] = [ahead, back]
        late = [step(ahead[: nodes // 2], 1), step(back[nodes // 2 :], -1)]
        totals = accumulate((dense, sibling), totals, ready, chunks[ready:])
        mixed = call(
            attend_kernel,
            sds((nodes, width), F32),
            [SMEM] + [VMEM] * 9,
            (me, features, qfeat, gate, quarter, flip(quarter, 2), flip(quarter, 1), flip(quarter, 3), w_out, totals[0]),
        )
        late = after(late, *totals, mixed)
        start = len(chunks)
        (given,) = accumulate((sibling,), totals[1:], start, late, BF16)
        (mine,) = accumulate((dense,), [mixed], start, late)
        theirs = flip(given, 1)

        def final_kernel(mine_ref, theirs_ref, gain_ref, up_ref, down_ref, out_ref):
            mixed = mine_ref[...] + theirs_ref[...].astype(F32)
            second = layer_norm(mixed, gain_ref[...])
            inner = jnp.maximum(dot(second, up_ref[...]), 0.0).astype(BF16)
            out_ref[...] = (mixed + dot(inner, down_ref[...])).astype(BF16)

        return call(
            final_kernel,
            sds((nodes, width), BF16),
            [VMEM] * 5,
            (mine, theirs, ln2_gain.reshape(1, width), w_up, w_down),
        )

    split_rows = P(("groups", "blk"))
    return jax.shard_map(
        on_device,
        mesh=mesh,
        in_specs=(split_rows,) * 5 + (P(),) * 11,
        out_specs=P(("groups", "blk"), None),
        check_vma=False,
    )


def chip_order(mesh, size):
    devices = mesh.devices.reshape(-1, size)[0]
    coords = [getattr(d, "coords", None) for d in devices[::2]]
    if any(c is None for c in coords) or len({c[1] for c in map(tuple, coords)}) != 2:
        return list(range(size // 2))
    low = min(c[1] for c in coords)
    up = sorted((i for i, c in enumerate(coords) if c[1] == low), key=lambda i: coords[i][2])
    down = sorted((i for i, c in enumerate(coords) if c[1] != low), key=lambda i: -coords[i][2])
    return up + down
```

```python
import jax
import jax.numpy as jnp
from jax import lax
from jax.experimental import pallas as pl
from jax.experimental.pallas import tpu as pltpu
from jax.sharding import PartitionSpec as P

HEADS = 8
EPS = 1e-05
F32 = jnp.float32
BF16 = jnp.bfloat16
VMEM = pl.BlockSpec(memory_space=pltpu.VMEM)
SMEM = pl.BlockSpec(memory_space=pltpu.SMEM)
HBM = pl.BlockSpec(memory_space=pltpu.HBM)


def dot(a, b):
    return jnp.dot(a, b, preferred_element_type=F32)


def split(value):
    high = value.astype(BF16)
    return high, (value - high.astype(F32)).astype(BF16)


def layer_norm(values, gain):
    mean = jnp.mean(values, axis=-1, keepdims=True)
    centered = values - mean
    var = jnp.mean(centered * centered, axis=-1, keepdims=True)
    return (centered * lax.rsqrt(var + EPS) * gain).astype(BF16)


def call(body, outs, specs, args, scratch=(), limit=None):
    held = sum(a.size * a.dtype.itemsize for a in (*args, *jax.tree.leaves(outs)))
    limit = limit or held // 2**20 + 7
    return pl.pallas_call(
        body,
        out_shape=outs,
        in_specs=specs,
        out_specs=jax.tree.map(lambda _: VMEM, outs),
        scratch_shapes=scratch,
        compiler_params=pltpu.CompilerParams(vmem_limit_bytes=int(limit * 2**20)),
        cost_estimate=pl.CostEstimate(flops=1, bytes_accessed=1, transcendentals=0),
    )(*args)


def after(values, *others):
    any_space = pl.BlockSpec(memory_space=pl.ANY)
    return pl.pallas_call(
        lambda *refs: None,
        out_shape=[sds(v.shape, v.dtype) for v in values],
        in_specs=[any_space] * (len(values) + len(others)),
        out_specs=[any_space] * len(values),
        input_output_aliases={i: i for i in range(len(values))},
        compiler_params=pltpu.CompilerParams(vmem_limit_bytes=2**20),
        cost_estimate=pl.CostEstimate(flops=1, bytes_accessed=1, transcendentals=0),
    )(*values, *others)


def sds(shape, dtype):
    return jax.ShapeDtypeStruct(shape, dtype)


def pair_ones(rows, lanes):
    top = lax.broadcasted_iota(jnp.int32, (rows, lanes), 0) < rows // 2
    left = lax.broadcasted_iota(jnp.int32, (rows, lanes), 1) < lanes // 2
    return jnp.where(top == left, 1.0, 0.0)


def pair_omega(omega):
    zero = jnp.zeros_like(omega)
    return jnp.concatenate(
        [jnp.concatenate([omega, zero], axis=1), jnp.concatenate([zero, omega], axis=1)], axis=0
    )


class Fetch:
    def __init__(self, source, target, sems, pieces):
        rows = source.shape[0] // pieces
        self.copies = [
            pltpu.make_async_copy(
                source.at[pl.ds(i * rows, rows)], target.at[pl.ds(i * rows, rows)], sems.at[i]
            )
            for i in range(pieces)
        ]
        for copy in self.copies:
            copy.start()

    def wait(self):
        for copy in self.copies:
            copy.wait()


def buffers(*fetches):
    return [pltpu.VMEM(a.shape, a.dtype) for a, _ in fetches] + [
        pltpu.SemaphoreType.DMA((pieces,)) for _, pieces in fetches
    ]


PIECES = 4
EXTRA = 56


def message_kernel(
    x_hbm, gain_hbm, w_hbm, normed_ref, msg_ref, x_ref, gain_ref, w_ref, x_sem, gain_sem, w_sem
):
    x_copy = Fetch(x_hbm, x_ref, x_sem, PIECES)
    gain_copy = Fetch(gain_hbm, gain_ref, gain_sem, 1)
    w_copy = Fetch(w_hbm, w_ref, w_sem, PIECES)
    gain_copy.wait()
    x_copy.wait()
    normed = layer_norm(x_ref[...].astype(F32), gain_ref[...])
    normed_ref[...] = normed
    w_copy.wait()
    msg_ref[...] = dot(normed, w_ref[...]).astype(BF16)


def kv_kernel(
    normed_hbm, wk_hbm, wv_hbm, omega_hbm, own_ref, near_ref, core_ref, both_ref, sums_ref,
    normed_ref, wk_ref, wv_ref, omega_ref, normed_sem, wk_sem, wv_sem, omega_sem
):
    normed_copy = Fetch(normed_hbm, normed_ref, normed_sem, PIECES)
    wk_copy = Fetch(wk_hbm, wk_ref, wk_sem, PIECES)
    omega_copy = Fetch(omega_hbm, omega_ref, omega_sem, 1)
    wv_copy = Fetch(wv_hbm, wv_ref, wv_sem, PIECES)
    width = normed_ref.shape[1]
    head = width // HEADS
    feat = omega_ref.shape[1]
    normed_copy.wait()
    normed = normed_ref[...]
    wk_copy.wait()
    keys = dot(normed, wk_ref[...]) * (head ** (-0.25))
    omega_copy.wait()
    wv_copy.wait()
    values = dot(normed, wv_ref[...])
    high, low = split(pair_omega(omega_ref[...]))
    ones = (-0.5 * pair_ones(2 * head, 2 * feat)).astype(BF16)
    first = jnp.concatenate([high, high], axis=0)
    second = jnp.concatenate([low, ones, ones], axis=0)
    left = lax.broadcasted_iota(jnp.int32, (feat, 2 * head), 1) < head
    pad = jnp.zeros((own_ref.shape[0] - feat - 2, feat), F32)
    for pair in range(HEADS // 2):
        k_pair = keys[:, pair * 2 * head : (pair + 1) * 2 * head]
        k_high, k_low = split(k_pair)
        s_high, s_low = split(k_pair * k_pair)
        logits = dot(jnp.concatenate([k_high, k_low], axis=1), first) + dot(
            jnp.concatenate([k_high, s_high, s_low], axis=1), second
        )
        kfeat = jnp.exp(logits)
        total = jnp.sum(kfeat, axis=0, keepdims=True)
        f_high, f_low = split(kfeat)
        v_high, v_low = split(values[:, pair * 2 * head : (pair + 1) * 2 * head])
        dims = (((0,), (0,)), ((), ()))
        both = lax.dot_general(f_high, v_high, dims, preferred_element_type=F32)
        both += lax.dot_general(f_low, v_high, dims, preferred_element_type=F32)
        both += lax.dot_general(f_high, v_low, dims, preferred_element_type=F32)
        block = jnp.where(left, both[:feat], both[feat:])
        sums_ref[pair] = jnp.concatenate([block, total[:, :feat], total[:, feat:], pad], axis=0)
    me = lax.axis_index("blk")
    mine = (me % 2) * 2 + (me // 2) % 2
    own_ref[...] = sums_ref[mine]
    near_ref[...] = sums_ref[mine ^ 1].astype(BF16)
    core_ref[...] = sums_ref[mine ^ 2].astype(BF16)
    both_ref[...] = sums_ref[mine ^ 3].astype(BF16)


def query_kernel(normed_ref, wq_ref, wg_ref, omega_ref, qf_ref, gate_ref):
    normed = normed_ref[...]
    width = normed.shape[1]
    head = width // HEADS
    feat = omega_ref.shape[1]
    query = dot(normed, wq_ref[...]) * (head ** (-0.25))
    high, low = split(pair_omega(omega_ref[...]))
    first = jnp.concatenate([high, high], axis=0)
    for pair in range(HEADS // 2):
        q_high, q_low = split(query[:, pair * 2 * head : (pair + 1) * 2 * head])
        logits = dot(jnp.concatenate([q_high, q_low], axis=1), first) + dot(q_high, low)
        qf_ref[:, pair * 2 * feat : (pair + 1) * 2 * feat] = jnp.exp(logits).astype(BF16)
    gate_ref[...] = jax.nn.sigmoid(dot(normed, wg_ref[...]))


def place_kernel(core_ref, rows_ref, cols_ref, count_ref, tiles_ref, before_ref, mine_ref, theirs_ref):
    del before_ref
    per = mine_ref.shape[1]
    mine_ref[...] = jnp.zeros_like(mine_ref)
    theirs_ref[...] = jnp.zeros_like(theirs_ref)

    def body(slot, carry):
        col, row = cols_ref[slot], rows_ref[slot]
        place = (col // (2 * per)) * per + col % per
        own = (col // per) % 2 == core_ref[0]

        @pl.when(own)
        def _():
            mine_ref[place, row] = tiles_ref[slot]

        @pl.when(jnp.logical_not(own))
        def _():
            theirs_ref[place, row] = tiles_ref[slot]

        return carry

    lax.fori_loop(0, count_ref[0], body, 0)


def attend_kernel(
    x_ref, qf_ref, gate_ref, own_ref, pair_ref, core_ref, both_ref, wo_ref, total_ref, mixed_ref
):
    width = x_ref.shape[1]
    head = width // HEADS
    feat = own_ref.shape[1]
    me = lax.axis_index("blk")
    mine = (me % 2) * 2 + (me // 2) % 2
    left = lax.broadcasted_iota(jnp.int32, (feat, 2 * head), 1) < head
    ones = pair_ones(2 * feat, 2 * head).astype(BF16)
    joined = []
    for pair in range(HEADS // 2):
        offset = mine ^ pair
        part = own_ref[...].astype(F32)
        for other, ref in ((1, pair_ref), (2, core_ref), (3, both_ref)):
            part = jnp.where(offset == other, ref[...].astype(F32), part)
        block = part[:feat]
        block = jnp.concatenate([jnp.where(left, block, 0.0), jnp.where(left, 0.0, block)], axis=0)
        ksum = jnp.concatenate([part[feat : feat + 1], part[feat + 1 : feat + 2]], axis=1)
        q_pair = qf_ref[:, pair * 2 * feat : (pair + 1) * 2 * feat]
        numer = dot(q_pair, block.astype(BF16))
        d_high, d_low = split(q_pair.astype(F32) * ksum)
        denom = dot(d_high, ones) + dot(d_low, ones)
        joined.append(numer / denom)
    attn = jnp.concatenate(joined, axis=1)
    gated = (attn * gate_ref[...]).astype(BF16)
    mixed_ref[...] = x_ref[...].astype(F32) + total_ref[...] + dot(gated, wo_ref[...])


def columns(dense_ref, column, count):
    rows, tile = dense_ref.shape[1:3]
    weights = [
        jnp.concatenate([dense_ref[column + col, row] for col in range(count // tile)], axis=1)
        for row in range(rows)
    ]
    return jnp.concatenate(weights, axis=0)


def late_kernel(total_ref, weights_ref, upper_ref, lower_ref, out_ref):
    rows = jnp.concatenate([upper_ref[...], lower_ref[...]], axis=0)
    out_ref[...] = (total_ref[...] + dot(weights_ref[...], rows)).astype(out_ref.dtype)


def solution(mesh):
    size = mesh.shape["blk"]
    chips = size // 2
    order = chip_order(mesh, size)

    def step(value, shift):
        pairs = [
            (order[p] * 2 + c, order[(p + shift) % chips] * 2 + c)
            for p in range(chips)
            for c in range(2)
        ]
        return lax.ppermute(value, "blk", pairs)

    def flip(value, bit):
        return lax.ppermute(value, "blk", [(i, i ^ bit) for i in range(size)])

    def on_device(
        features,
        tiles,
        block_rows,
        block_cols,
        block_count,
        ln_gain,
        w_msg,
        w_query,
        w_key,
        w_value,
        w_gate,
        w_out,
        omega,
        ln2_gain,
        w_up,
        w_down,
    ):
        nodes, width = features.shape
        tile = tiles.shape[1]
        feat = omega.shape[1]
        head = width // HEADS
        row_blocks = nodes // tile
        me = lax.axis_index("blk")
        core = (me % 2).reshape(1)
        me = me.reshape(1)
        normed, message = call(
            message_kernel,
            (sds((nodes, width), BF16), sds((nodes, width), BF16)),
            [HBM] * 3,
            (features, ln_gain.reshape(1, width), w_msg),
            buffers((features, PIECES), (sds((1, width), F32), 1), (w_msg, PIECES)),
            EXTRA,
        )

        full = (chips - 1) // 2
        ahead, back = step(message, 1), step(message, -1)

        rows = feat + 16
        given = sds((rows, feat), BF16)
        own, near, across, both = call(
            kv_kernel,
            (sds((rows, feat), F32), given, given, given),
            [HBM] * 4,
            (normed, w_key, w_value, omega),
            [pltpu.VMEM((HEADS // 2, rows, feat), F32)]
            + buffers((normed, PIECES), (w_key, PIECES), (w_value, PIECES), (omega, 1)),
            56,
        )
        ahead, back = after([ahead, back], near)
        sums = [sum((flip(v, b).astype(F32) for v, b in ((near, 2), (across, 1), (both, 3))), own)]
        bit = 4
        while bit < size:
            hops = [bit, 2 * bit, 3 * bit] if 2 * bit < size else [bit]
            sent = sums[-1].astype(BF16)
            sums.append(sum((flip(sent, hop).astype(F32) for hop in hops), sums[-1]))
            bit *= 4
        quarter = sums[-1].astype(BF16)

        qfeat, gate = call(
            query_kernel,
            (sds((nodes, HEADS * feat), BF16), sds((nodes, width), F32)),
            [VMEM] * 4,
            (normed, w_query, w_gate, omega),
        )
        blocks = sds((chips * row_blocks, row_blocks, tile, tile), BF16)
        dense, others = call(
            place_kernel,
            (blocks, blocks),
            [SMEM] * 4 + [VMEM, pl.BlockSpec(memory_space=pl.ANY)],
            (core, block_rows, block_cols, block_count, tiles, sums[0]),
        )
        shifts = [0] + [sign * k for k in range(1, full + 1) for sign in (1, -1)]
        if chips % 2 == 0:
            shifts += [chips // 2]
        home = {chip: p for p, chip in enumerate(order)}

        def lookup(values, index):
            return sum(jnp.where(index == i, value, 0) for i, value in enumerate(values))

        def accumulate(totals, first, chunks, aside=None):
            totals = list(totals)

            def body(mine_ref, sibling_ref, *refs):
                place_here = lookup([home[c] for c in range(chips)], lax.axis_index("blk") // 2)
                chunk_refs = refs[len(totals) : len(totals) + len(chunks)]
                outs = refs[len(totals) + len(chunks) :]

                def weights(dense_ref, place):
                    chip = lookup(order, lax.rem(place_here - shifts[place] + 2 * chips, chips))
                    return columns(dense_ref, chip * row_blocks, nodes)

                for i, dense_ref in enumerate((mine_ref, sibling_ref)):
                    value = refs[i][...] if totals else None
                    for place, chunk_ref in enumerate(chunk_refs):
                        part = dot(weights(dense_ref, first + place), chunk_ref[...])
                        value = part if value is None else value + part
                    outs[i][...] = value
                    if aside is not None:
                        outs[2 + i][...] = weights(dense_ref, aside)

            outs = [sds((nodes, width), F32)] * 2
            if aside is not None:
                outs += [sds((nodes, nodes), BF16)] * 2
            return call(
                body,
                outs,
                [VMEM] * (2 + len(totals) + len(chunks)),
                (dense, sibling, *totals, *chunks),
            )

        chunks = [message, ahead, back]
        totals, used = (), 0
        sibling = None
        for k in range(2, full + 1):
            if k == 3:
                ahead, back, others = after([ahead, back, others], dense)
                chunks[-2:] = [ahead, back]
                sibling = flip(others, 1)
            if k > 3:
                ready = 1 + 2 * (k - 2)
                totals = accumulate(totals, used, chunks[used:ready])
                used = ready
                ahead, back = after([ahead, back], totals[0])
                chunks[-2:] = [ahead, back]
            ahead, back = step(ahead, 1), step(back, -1)
            chunks += [ahead, back]
        ready = 1 + 2 * (full - 1)
        totals = accumulate(totals, used, chunks[used:ready])
        ahead, back = after([ahead, back], totals[0], qfeat)
        chunks[-2:] = [ahead, back]
        late = [step(ahead[: nodes // 2], 1), step(back[nodes // 2 :], -1)]
        *totals, mine_late, sibling_late = accumulate(totals, ready, chunks[ready:], len(chunks))
        gathered = [flip(quarter, bits) for bits in (2, 1, 3)]
        mixed = call(
            attend_kernel,
            sds((nodes, width), F32),
            [VMEM] * 9,
            (features, qfeat, gate, quarter, *gathered, w_out, totals[0]),
        )
        late = after(late, *totals, *gathered)
        late_given, late_mine = sds((nodes, width), BF16), sds((nodes, width), F32)
        given = call(late_kernel, late_given, [VMEM] * 4, (totals[1], sibling_late, *late))
        mine = call(late_kernel, late_mine, [VMEM] * 4, (mixed, mine_late, *late))
        theirs = flip(given, 1)

        def final_kernel(mine_ref, theirs_ref, gain_ref, up_ref, down_ref, out_ref):
            mixed = mine_ref[...] + theirs_ref[...].astype(F32)
            second = layer_norm(mixed, gain_ref[...])
            inner = jnp.maximum(dot(second, up_ref[...]), 0.0).astype(BF16)
            out_ref[...] = (mixed + dot(inner, down_ref[...])).astype(BF16)

        return call(
            final_kernel,
            sds((nodes, width), BF16),
            [VMEM] * 5,
            (mine, theirs, ln2_gain.reshape(1, width), w_up, w_down),
        )

    split_rows = P(("groups", "blk"))
    return jax.shard_map(
        on_device,
        mesh=mesh,
        in_specs=(split_rows,) * 5 + (P(),) * 11,
        out_specs=P(("groups", "blk"), None),
        check_vma=False,
    )


def chip_order(mesh, size):
    devices = mesh.devices.reshape(-1, size)[0]
    coords = [getattr(d, "coords", None) for d in devices[::2]]
    if any(c is None for c in coords) or len({c[1] for c in map(tuple, coords)}) != 2:
        return list(range(size // 2))
    low = min(c[1] for c in coords)
    up = sorted((i for i, c in enumerate(coords) if c[1] == low), key=lambda i: coords[i][2])
    down = sorted((i for i, c in enumerate(coords) if c[1] != low), key=lambda i: -coords[i][2])
    return up + down
```

```python
import jax
import jax.numpy as jnp
from jax import lax
from jax.experimental import pallas as pl
from jax.experimental.pallas import tpu as pltpu
from jax.sharding import PartitionSpec as P

HEADS = 8
EPS = 1e-05
F32 = jnp.float32
BF16 = jnp.bfloat16
VMEM = pl.BlockSpec(memory_space=pltpu.VMEM)
SMEM = pl.BlockSpec(memory_space=pltpu.SMEM)
HBM = pl.BlockSpec(memory_space=pltpu.HBM)


def dot(a, b):
    return jnp.dot(a, b, preferred_element_type=F32)


def split(value):
    high = value.astype(BF16)
    return high, (value - high.astype(F32)).astype(BF16)


def layer_norm(values, gain):
    mean = jnp.mean(values, axis=-1, keepdims=True)
    centered = values - mean
    var = jnp.mean(centered * centered, axis=-1, keepdims=True)
    return (centered * lax.rsqrt(var + EPS) * gain).astype(BF16)


def call(body, outs, specs, args, scratch=(), limit=None):
    held = sum(a.size * a.dtype.itemsize for a in (*args, *jax.tree.leaves(outs)))
    limit = limit or held // 2**20 + 7
    return pl.pallas_call(
        body,
        out_shape=outs,
        in_specs=specs,
        out_specs=jax.tree.map(lambda o: SMEM if o.shape == (1,) else VMEM, outs),
        scratch_shapes=scratch,
        compiler_params=pltpu.CompilerParams(vmem_limit_bytes=int(limit * 2**20)),
        cost_estimate=pl.CostEstimate(flops=1, bytes_accessed=1, transcendentals=0),
    )(*args)


def after(values, *others):
    any_space = pl.BlockSpec(memory_space=pl.ANY)
    return pl.pallas_call(
        lambda *refs: None,
        out_shape=[sds(v.shape, v.dtype) for v in values],
        in_specs=[SMEM if v.shape == (1,) else any_space for v in (*values, *others)],
        out_specs=[any_space] * len(values),
        input_output_aliases={i: i for i in range(len(values))},
        compiler_params=pltpu.CompilerParams(vmem_limit_bytes=2**20),
        cost_estimate=pl.CostEstimate(flops=1, bytes_accessed=1, transcendentals=0),
    )(*values, *others)


def sds(shape, dtype):
    return jax.ShapeDtypeStruct(shape, dtype)


def pair_ones(rows, lanes):
    top = lax.broadcasted_iota(jnp.int32, (rows, lanes), 0) < rows // 2
    left = lax.broadcasted_iota(jnp.int32, (rows, lanes), 1) < lanes // 2
    return jnp.where(top == left, 1.0, 0.0)


def pair_omega(omega):
    zero = jnp.zeros_like(omega)
    return jnp.concatenate(
        [jnp.concatenate([omega, zero], axis=1), jnp.concatenate([zero, omega], axis=1)], axis=0
    )


class Fetch:
    def __init__(self, source, target, sems, pieces):
        rows = source.shape[0] // pieces
        self.copies = [
            pltpu.make_async_copy(
                source.at[pl.ds(i * rows, rows)], target.at[pl.ds(i * rows, rows)], sems.at[i]
            )
            for i in range(pieces)
        ]
        for copy in self.copies:
            copy.start()

    def wait(self):
        for copy in self.copies:
            copy.wait()


def buffers(*fetches):
    return [pltpu.VMEM(a.shape, a.dtype) for a, _ in fetches] + [
        pltpu.SemaphoreType.DMA((pieces,)) for _, pieces in fetches
    ]


PIECES = 4
EXTRA = 56


def message_kernel(
    x_hbm, gain_hbm, w_hbm, normed_ref, msg_ref, x_ref, gain_ref, w_ref, x_sem, gain_sem, w_sem
):
    x_copy = Fetch(x_hbm, x_ref, x_sem, PIECES)
    gain_copy = Fetch(gain_hbm, gain_ref, gain_sem, 1)
    w_copy = Fetch(w_hbm, w_ref, w_sem, PIECES)
    gain_copy.wait()
    x_copy.wait()
    normed = layer_norm(x_ref[...].astype(F32), gain_ref[...])
    normed_ref[...] = normed
    w_copy.wait()
    msg_ref[...] = dot(normed, w_ref[...]).astype(BF16)


def kv_kernel(
    normed_hbm, wk_hbm, wv_hbm, omega_hbm, own_ref, near_ref, core_ref, both_ref, done_ref, sums_ref,
    normed_ref, wk_ref, wv_ref, omega_ref, normed_sem, wk_sem, wv_sem, omega_sem
):
    normed_copy = Fetch(normed_hbm, normed_ref, normed_sem, PIECES)
    wk_copy = Fetch(wk_hbm, wk_ref, wk_sem, PIECES)
    omega_copy = Fetch(omega_hbm, omega_ref, omega_sem, 1)
    wv_copy = Fetch(wv_hbm, wv_ref, wv_sem, PIECES)
    width = normed_ref.shape[1]
    head = width // HEADS
    feat = omega_ref.shape[1]
    normed_copy.wait()
    normed = normed_ref[...]
    wk_copy.wait()
    keys = dot(normed, wk_ref[...]) * (head ** (-0.25))
    omega_copy.wait()
    wv_copy.wait()
    values = dot(normed, wv_ref[...])
    high, low = split(pair_omega(omega_ref[...]))
    ones = (-0.5 * pair_ones(2 * head, 2 * feat)).astype(BF16)
    first = jnp.concatenate([high, high], axis=0)
    second = jnp.concatenate([low, ones, ones], axis=0)
    left = lax.broadcasted_iota(jnp.int32, (feat, 2 * head), 1) < head
    pad = jnp.zeros((own_ref.shape[0] - feat - 2, feat), F32)
    for pair in range(HEADS // 2):
        k_pair = keys[:, pair * 2 * head : (pair + 1) * 2 * head]
        k_high, k_low = split(k_pair)
        s_high, s_low = split(k_pair * k_pair)
        logits = dot(jnp.concatenate([k_high, k_low], axis=1), first) + dot(
            jnp.concatenate([k_high, s_high, s_low], axis=1), second
        )
        kfeat = jnp.exp(logits)
        total = jnp.sum(kfeat, axis=0, keepdims=True)
        f_high, f_low = split(kfeat)
        v_high, v_low = split(values[:, pair * 2 * head : (pair + 1) * 2 * head])
        dims = (((0,), (0,)), ((), ()))
        both = lax.dot_general(f_high, v_high, dims, preferred_element_type=F32)
        both += lax.dot_general(f_low, v_high, dims, preferred_element_type=F32)
        both += lax.dot_general(f_high, v_low, dims, preferred_element_type=F32)
        block = jnp.where(left, both[:feat], both[feat:])
        sums_ref[pair] = jnp.concatenate([block, total[:, :feat], total[:, feat:], pad], axis=0)
    me = lax.axis_index("blk")
    mine = (me % 2) * 2 + (me // 2) % 2
    own_ref[...] = sums_ref[mine]
    near_ref[...] = sums_ref[mine ^ 1].astype(BF16)
    core_ref[...] = sums_ref[mine ^ 2].astype(BF16)
    both_ref[...] = sums_ref[mine ^ 3].astype(BF16)
    done_ref[0] = mine


def query_kernel(normed_ref, wq_ref, wg_ref, omega_ref, qf_ref, gate_ref):
    normed = normed_ref[...]
    width = normed.shape[1]
    head = width // HEADS
    feat = omega_ref.shape[1]
    query = dot(normed, wq_ref[...]) * (head ** (-0.25))
    high, low = split(pair_omega(omega_ref[...]))
    first = jnp.concatenate([high, high], axis=0)
    for pair in range(HEADS // 2):
        q_high, q_low = split(query[:, pair * 2 * head : (pair + 1) * 2 * head])
        logits = dot(jnp.concatenate([q_high, q_low], axis=1), first) + dot(q_high, low)
        qf_ref[:, pair * 2 * feat : (pair + 1) * 2 * feat] = jnp.exp(logits).astype(BF16)
    gate_ref[...] = jax.nn.sigmoid(dot(normed, wg_ref[...]))


def place_kernel(core_ref, rows_ref, cols_ref, count_ref, tiles_ref, before_ref, mine_ref, theirs_ref):
    del before_ref
    per = mine_ref.shape[1]
    mine_ref[...] = jnp.zeros_like(mine_ref)
    theirs_ref[...] = jnp.zeros_like(theirs_ref)

    def body(slot, carry):
        col, row = cols_ref[slot], rows_ref[slot]
        place = (col // (2 * per)) * per + col % per
        own = (col // per) % 2 == core_ref[0]

        @pl.when(own)
        def _():
            mine_ref[place, row] = tiles_ref[slot]

        @pl.when(jnp.logical_not(own))
        def _():
            theirs_ref[place, row] = tiles_ref[slot]

        return carry

    lax.fori_loop(0, count_ref[0], body, 0)


def attend_kernel(
    x_ref, qf_ref, gate_ref, own_ref, pair_ref, core_ref, both_ref, wo_ref, total_ref, mixed_ref
):
    width = x_ref.shape[1]
    head = width // HEADS
    feat = own_ref.shape[1]
    me = lax.axis_index("blk")
    mine = (me % 2) * 2 + (me // 2) % 2
    left = lax.broadcasted_iota(jnp.int32, (feat, 2 * head), 1) < head
    ones = pair_ones(2 * feat, 2 * head).astype(BF16)
    joined = []
    for pair in range(HEADS // 2):
        offset = mine ^ pair
        part = own_ref[...].astype(F32)
        for other, ref in ((1, pair_ref), (2, core_ref), (3, both_ref)):
            part = jnp.where(offset == other, ref[...].astype(F32), part)
        block = part[:feat]
        block = jnp.concatenate([jnp.where(left, block, 0.0), jnp.where(left, 0.0, block)], axis=0)
        ksum = jnp.concatenate([part[feat : feat + 1], part[feat + 1 : feat + 2]], axis=1)
        q_pair = qf_ref[:, pair * 2 * feat : (pair + 1) * 2 * feat]
        numer = dot(q_pair, block.astype(BF16))
        d_high, d_low = split(q_pair.astype(F32) * ksum)
        denom = dot(d_high, ones) + dot(d_low, ones)
        joined.append(numer / denom)
    attn = jnp.concatenate(joined, axis=1)
    gated = (attn * gate_ref[...]).astype(BF16)
    mixed_ref[...] = x_ref[...].astype(F32) + total_ref[...] + dot(gated, wo_ref[...])


def columns(dense_ref, column, count):
    rows, tile = dense_ref.shape[1:3]
    weights = [
        jnp.concatenate([dense_ref[column + col, row] for col in range(count // tile)], axis=1)
        for row in range(rows)
    ]
    return jnp.concatenate(weights, axis=0)


def late_kernel(total_ref, weights_ref, upper_ref, lower_ref, out_ref):
    rows = jnp.concatenate([upper_ref[...], lower_ref[...]], axis=0)
    out_ref[...] = (total_ref[...] + dot(weights_ref[...], rows)).astype(out_ref.dtype)


def solution(mesh):
    size = mesh.shape["blk"]
    chips = size // 2
    order = chip_order(mesh, size)

    def step(value, shift):
        pairs = [
            (order[p] * 2 + c, order[(p + shift) % chips] * 2 + c)
            for p in range(chips)
            for c in range(2)
        ]
        return lax.ppermute(value, "blk", pairs)

    def flip(value, bit):
        return lax.ppermute(value, "blk", [(i, i ^ bit) for i in range(size)])

    def on_device(
        features,
        tiles,
        block_rows,
        block_cols,
        block_count,
        ln_gain,
        w_msg,
        w_query,
        w_key,
        w_value,
        w_gate,
        w_out,
        omega,
        ln2_gain,
        w_up,
        w_down,
    ):
        nodes, width = features.shape
        tile = tiles.shape[1]
        feat = omega.shape[1]
        head = width // HEADS
        row_blocks = nodes // tile
        me = lax.axis_index("blk")
        core = (me % 2).reshape(1)
        me = me.reshape(1)
        normed, message = call(
            message_kernel,
            (sds((nodes, width), BF16), sds((nodes, width), BF16)),
            [HBM] * 3,
            (features, ln_gain.reshape(1, width), w_msg),
            buffers((features, PIECES), (sds((1, width), F32), 1), (w_msg, PIECES)),
            EXTRA,
        )

        full = (chips - 1) // 2
        ahead, back = step(message, 1), step(message, -1)

        rows = feat + 16
        given = sds((rows, feat), BF16)
        own, near, across, both, done = call(
            kv_kernel,
            (sds((rows, feat), F32), given, given, given, sds((1,), jnp.int32)),
            [HBM] * 4,
            (normed, w_key, w_value, omega),
            [pltpu.VMEM((HEADS // 2, rows, feat), F32)]
            + buffers((normed, PIECES), (w_key, PIECES), (w_value, PIECES), (omega, 1)),
            56,
        )
        ahead, back = after([ahead, back], done)
        sums = [sum((flip(v, b).astype(F32) for v, b in ((near, 2), (across, 1), (both, 3))), own)]
        bit = 4
        while bit < size:
            hops = [3 * bit, 2 * bit, bit] if 2 * bit < size else [bit]
            sent = sums[-1].astype(BF16)
            sums.append(sum((flip(sent, hop).astype(F32) for hop in hops), sums[-1]))
            bit *= 4
        quarter = sums[-1].astype(BF16)

        qfeat, gate = call(
            query_kernel,
            (sds((nodes, HEADS * feat), BF16), sds((nodes, width), F32)),
            [VMEM] * 4,
            (normed, w_query, w_gate, omega),
        )
        blocks = sds((chips * row_blocks, row_blocks, tile, tile), BF16)
        dense, others = call(
            place_kernel,
            (blocks, blocks),
            [SMEM] * 4 + [VMEM, pl.BlockSpec(memory_space=pl.ANY)],
            (core, block_rows, block_cols, block_count, tiles, sums[0]),
        )
        shifts = [0] + [sign * k for k in range(1, full + 1) for sign in (1, -1)]
        if chips % 2 == 0:
            shifts += [chips // 2]
        home = {chip: p for p, chip in enumerate(order)}

        def lookup(values, index):
            return sum(jnp.where(index == i, value, 0) for i, value in enumerate(values))

        def accumulate(totals, first, chunks, aside=None):
            totals = list(totals)

            def body(mine_ref, sibling_ref, *refs):
                place_here = lookup([home[c] for c in range(chips)], lax.axis_index("blk") // 2)
                chunk_refs = refs[len(totals) : len(totals) + len(chunks)]
                outs = refs[len(totals) + len(chunks) :]

                def weights(dense_ref, place):
                    chip = lookup(order, lax.rem(place_here - shifts[place] + 2 * chips, chips))
                    return columns(dense_ref, chip * row_blocks, nodes)

                for i, dense_ref in enumerate((mine_ref, sibling_ref)):
                    value = refs[i][...] if totals else None
                    for place, chunk_ref in enumerate(chunk_refs):
                        part = dot(weights(dense_ref, first + place), chunk_ref[...])
                        value = part if value is None else value + part
                    outs[i][...] = value
                    if aside is not None:
                        outs[2 + i][...] = weights(dense_ref, aside)

            outs = [sds((nodes, width), F32)] * 2
            if aside is not None:
                outs += [sds((nodes, nodes), BF16)] * 2
            return call(
                body,
                outs,
                [VMEM] * (2 + len(totals) + len(chunks)),
                (dense, sibling, *totals, *chunks),
            )

        chunks = [message, ahead, back]
        totals, used = (), 0
        sibling = None
        for k in range(2, full + 1):
            if k == 3:
                ahead, back, others = after([ahead, back, others], dense)
                chunks[-2:] = [ahead, back]
                sibling = flip(others, 1)
            if k > 3:
                ready = 1 + 2 * (k - 2)
                totals = accumulate(totals, used, chunks[used:ready])
                used = ready
                ahead, back = after([ahead, back], totals[0])
                chunks[-2:] = [ahead, back]
            ahead, back = step(ahead, 1), step(back, -1)
            chunks += [ahead, back]
        ready = 1 + 2 * (full - 1)
        totals = accumulate(totals, used, chunks[used:ready])
        ahead, back = after([ahead, back], qfeat, totals[0])
        chunks[-2:] = [ahead, back]
        late = [step(ahead[: nodes // 2], 1), step(back[nodes // 2 :], -1)]
        *totals, mine_late, sibling_late = accumulate(totals, ready, chunks[ready:], len(chunks))
        gathered = [flip(quarter, bits) for bits in (2, 1, 3)]
        mixed = call(
            attend_kernel,
            sds((nodes, width), F32),
            [VMEM] * 9,
            (features, qfeat, gate, quarter, *gathered, w_out, totals[0]),
        )
        late = after(late, *totals, *gathered)
        late_given, late_mine = sds((nodes, width), BF16), sds((nodes, width), F32)
        given = call(late_kernel, late_given, [VMEM] * 4, (totals[1], sibling_late, *late))
        mine = call(late_kernel, late_mine, [VMEM] * 4, (mixed, mine_late, *late))
        theirs = flip(given, 1)

        def final_kernel(mine_ref, theirs_ref, gain_ref, up_ref, down_ref, out_ref):
            mixed = mine_ref[...] + theirs_ref[...].astype(F32)
            second = layer_norm(mixed, gain_ref[...])
            inner = jnp.maximum(dot(second, up_ref[...]), 0.0).astype(BF16)
            out_ref[...] = (mixed + dot(inner, down_ref[...])).astype(BF16)

        return call(
            final_kernel,
            sds((nodes, width), BF16),
            [VMEM] * 5,
            (mine, theirs, ln2_gain.reshape(1, width), w_up, w_down),
        )

    split_rows = P(("groups", "blk"))
    return jax.shard_map(
        on_device,
        mesh=mesh,
        in_specs=(split_rows,) * 5 + (P(),) * 11,
        out_specs=P(("groups", "blk"), None),
        check_vma=False,
    )


def chip_order(mesh, size):
    devices = mesh.devices.reshape(-1, size)[0]
    coords = [getattr(d, "coords", None) for d in devices[::2]]
    if any(c is None for c in coords) or len({c[1] for c in map(tuple, coords)}) != 2:
        return list(range(size // 2))
    low = min(c[1] for c in coords)
    up = sorted((i for i, c in enumerate(coords) if c[1] == low), key=lambda i: coords[i][2])
    down = sorted((i for i, c in enumerate(coords) if c[1] != low), key=lambda i: -coords[i][2])
    return up + down
```

```python
import jax
import jax.numpy as jnp
from jax import lax
from jax.experimental import pallas as pl
from jax.experimental.pallas import tpu as pltpu
from jax.sharding import PartitionSpec as P

HEADS = 8
EPS = 1e-05
F32 = jnp.float32
BF16 = jnp.bfloat16
VMEM = pl.BlockSpec(memory_space=pltpu.VMEM)
SMEM = pl.BlockSpec(memory_space=pltpu.SMEM)
HBM = pl.BlockSpec(memory_space=pltpu.HBM)


def dot(a, b):
    return jnp.dot(a, b, preferred_element_type=F32)


def split(value):
    high = value.astype(BF16)
    return high, (value - high.astype(F32)).astype(BF16)


def layer_norm(values, gain):
    mean = jnp.mean(values, axis=-1, keepdims=True)
    centered = values - mean
    var = jnp.mean(centered * centered, axis=-1, keepdims=True)
    return (centered * lax.rsqrt(var + EPS) * gain).astype(BF16)


def call(body, outs, specs, args, scratch=(), limit=None):
    held = sum(a.size * a.dtype.itemsize for a in (*args, *jax.tree.leaves(outs)))
    limit = limit or held // 2**20 + 7
    return pl.pallas_call(
        body,
        out_shape=outs,
        in_specs=specs,
        out_specs=jax.tree.map(lambda o: SMEM if o.shape == (1,) else VMEM, outs),
        scratch_shapes=scratch,
        compiler_params=pltpu.CompilerParams(vmem_limit_bytes=int(limit * 2**20)),
        cost_estimate=pl.CostEstimate(flops=1, bytes_accessed=1, transcendentals=0),
    )(*args)


def after(values, *others):
    any_space = pl.BlockSpec(memory_space=pl.ANY)
    return pl.pallas_call(
        lambda *refs: None,
        out_shape=[sds(v.shape, v.dtype) for v in values],
        in_specs=[SMEM if v.shape == (1,) else any_space for v in (*values, *others)],
        out_specs=[any_space] * len(values),
        input_output_aliases={i: i for i in range(len(values))},
        compiler_params=pltpu.CompilerParams(vmem_limit_bytes=2**20),
        cost_estimate=pl.CostEstimate(flops=1, bytes_accessed=1, transcendentals=0),
    )(*values, *others)


def sds(shape, dtype):
    return jax.ShapeDtypeStruct(shape, dtype)


def pair_ones(rows, lanes):
    top = lax.broadcasted_iota(jnp.int32, (rows, lanes), 0) < rows // 2
    left = lax.broadcasted_iota(jnp.int32, (rows, lanes), 1) < lanes // 2
    return jnp.where(top == left, 1.0, 0.0)


def pair_omega(omega):
    zero = jnp.zeros_like(omega)
    return jnp.concatenate(
        [jnp.concatenate([omega, zero], axis=1), jnp.concatenate([zero, omega], axis=1)], axis=0
    )


class Fetch:
    def __init__(self, source, target, sems, pieces):
        rows = source.shape[0] // pieces
        self.copies = [
            pltpu.make_async_copy(
                source.at[pl.ds(i * rows, rows)], target.at[pl.ds(i * rows, rows)], sems.at[i]
            )
            for i in range(pieces)
        ]
        for copy in self.copies:
            copy.start()

    def wait(self):
        for copy in self.copies:
            copy.wait()


def buffers(*fetches):
    return [pltpu.VMEM(a.shape, a.dtype) for a, _ in fetches] + [
        pltpu.SemaphoreType.DMA((pieces,)) for _, pieces in fetches
    ]


PIECES = 4
EXTRA = 56


def message_kernel(
    x_hbm, gain_hbm, w_hbm, normed_ref, msg_ref, x_ref, gain_ref, w_ref, x_sem, gain_sem, w_sem
):
    x_copy = Fetch(x_hbm, x_ref, x_sem, PIECES)
    gain_copy = Fetch(gain_hbm, gain_ref, gain_sem, 1)
    w_copy = Fetch(w_hbm, w_ref, w_sem, PIECES)
    gain_copy.wait()
    x_copy.wait()
    normed = layer_norm(x_ref[...].astype(F32), gain_ref[...])
    normed_ref[...] = normed
    w_copy.wait()
    msg_ref[...] = dot(normed, w_ref[...]).astype(BF16)


def kv_kernel(
    normed_hbm, wk_hbm, wv_hbm, omega_hbm, own_ref, near_ref, core_ref, both_ref, done_ref, sums_ref,
    normed_ref, wk_ref, wv_ref, omega_ref, normed_sem, wk_sem, wv_sem, omega_sem
):
    normed_copy = Fetch(normed_hbm, normed_ref, normed_sem, PIECES)
    wk_copy = Fetch(wk_hbm, wk_ref, wk_sem, PIECES)
    omega_copy = Fetch(omega_hbm, omega_ref, omega_sem, 1)
    wv_copy = Fetch(wv_hbm, wv_ref, wv_sem, PIECES)
    width = normed_ref.shape[1]
    head = width // HEADS
    feat = omega_ref.shape[1]
    normed_copy.wait()
    normed = normed_ref[...]
    wk_copy.wait()
    keys = dot(normed, wk_ref[...]) * (head ** (-0.25))
    omega_copy.wait()
    wv_copy.wait()
    values = dot(normed, wv_ref[...])
    high, low = split(pair_omega(omega_ref[...]))
    ones = (-0.5 * pair_ones(2 * head, 2 * feat)).astype(BF16)
    first = jnp.concatenate([high, high], axis=0)
    second = jnp.concatenate([low, ones, ones], axis=0)
    left = lax.broadcasted_iota(jnp.int32, (feat, 2 * head), 1) < head
    pad = jnp.zeros((own_ref.shape[0] - feat - 2, feat), F32)
    for pair in range(HEADS // 2):
        k_pair = keys[:, pair * 2 * head : (pair + 1) * 2 * head]
        k_high, k_low = split(k_pair)
        s_high, s_low = split(k_pair * k_pair)
        logits = dot(jnp.concatenate([k_high, k_low], axis=1), first) + dot(
            jnp.concatenate([k_high, s_high, s_low], axis=1), second
        )
        kfeat = jnp.exp(logits)
        total = jnp.sum(kfeat, axis=0, keepdims=True)
        f_high, f_low = split(kfeat)
        v_high, v_low = split(values[:, pair * 2 * head : (pair + 1) * 2 * head])
        dims = (((0,), (0,)), ((), ()))
        both = lax.dot_general(f_high, v_high, dims, preferred_element_type=F32)
        both += lax.dot_general(f_low, v_high, dims, preferred_element_type=F32)
        both += lax.dot_general(f_high, v_low, dims, preferred_element_type=F32)
        block = jnp.where(left, both[:feat], both[feat:])
        sums_ref[pair] = jnp.concatenate([block, total[:, :feat], total[:, feat:], pad], axis=0)
    me = lax.axis_index("blk")
    mine = (me % 2) * 2 + (me // 2) % 2
    own_ref[...] = sums_ref[mine]
    near_ref[...] = sums_ref[mine ^ 1].astype(BF16)
    core_ref[...] = sums_ref[mine ^ 2].astype(BF16)
    both_ref[...] = sums_ref[mine ^ 3].astype(BF16)
    done_ref[0] = mine


def query_kernel(normed_ref, wq_ref, wg_ref, omega_ref, qf_ref, gate_ref):
    normed = normed_ref[...]
    width = normed.shape[1]
    head = width // HEADS
    feat = omega_ref.shape[1]
    query = dot(normed, wq_ref[...]) * (head ** (-0.25))
    high, low = split(pair_omega(omega_ref[...]))
    first = jnp.concatenate([high, high], axis=0)
    for pair in range(HEADS // 2):
        q_high, q_low = split(query[:, pair * 2 * head : (pair + 1) * 2 * head])
        logits = dot(jnp.concatenate([q_high, q_low], axis=1), first) + dot(q_high, low)
        qf_ref[:, pair * 2 * feat : (pair + 1) * 2 * feat] = jnp.exp(logits).astype(BF16)
    gate_ref[...] = jax.nn.sigmoid(dot(normed, wg_ref[...]))


def place_kernel(core_ref, rows_ref, cols_ref, count_ref, tiles_ref, before_ref, mine_ref, theirs_ref):
    del before_ref
    per = mine_ref.shape[1]
    mine_ref[...] = jnp.zeros_like(mine_ref)
    theirs_ref[...] = jnp.zeros_like(theirs_ref)

    def body(slot, carry):
        col, row = cols_ref[slot], rows_ref[slot]
        place = (col // (2 * per)) * per + col % per
        own = (col // per) % 2 == core_ref[0]

        @pl.when(own)
        def _():
            mine_ref[place, row] = tiles_ref[slot]

        @pl.when(jnp.logical_not(own))
        def _():
            theirs_ref[place, row] = tiles_ref[slot]

        return carry

    lax.fori_loop(0, count_ref[0], body, 0)


def attend_kernel(
    x_ref, qf_ref, gate_ref, own_ref, pair_ref, core_ref, both_ref, wo_ref, total_ref, mixed_ref
):
    width = x_ref.shape[1]
    head = width // HEADS
    feat = own_ref.shape[1]
    me = lax.axis_index("blk")
    mine = (me % 2) * 2 + (me // 2) % 2
    left = lax.broadcasted_iota(jnp.int32, (feat, 2 * head), 1) < head
    ones = pair_ones(2 * feat, 2 * head).astype(BF16)
    joined = []
    for pair in range(HEADS // 2):
        offset = mine ^ pair
        part = own_ref[...].astype(F32)
        for other, ref in ((1, pair_ref), (2, core_ref), (3, both_ref)):
            part = jnp.where(offset == other, ref[...].astype(F32), part)
        block = part[:feat]
        block = jnp.concatenate([jnp.where(left, block, 0.0), jnp.where(left, 0.0, block)], axis=0)
        ksum = jnp.concatenate([part[feat : feat + 1], part[feat + 1 : feat + 2]], axis=1)
        q_pair = qf_ref[:, pair * 2 * feat : (pair + 1) * 2 * feat]
        numer = dot(q_pair, block.astype(BF16))
        d_high, d_low = split(q_pair.astype(F32) * ksum)
        denom = dot(d_high, ones) + dot(d_low, ones)
        joined.append(numer / denom)
    attn = jnp.concatenate(joined, axis=1)
    gated = (attn * gate_ref[...]).astype(BF16)
    mixed_ref[...] = x_ref[...].astype(F32) + total_ref[...] + dot(gated, wo_ref[...])


def columns(dense_ref, column, count):
    rows, tile = dense_ref.shape[1:3]
    weights = [
        jnp.concatenate([dense_ref[column + col, row] for col in range(count // tile)], axis=1)
        for row in range(rows)
    ]
    return jnp.concatenate(weights, axis=0)


def late_kernel(total_ref, weights_ref, upper_ref, lower_ref, out_ref):
    rows = jnp.concatenate([upper_ref[...], lower_ref[...]], axis=0)
    out_ref[...] = (total_ref[...] + dot(weights_ref[...], rows)).astype(out_ref.dtype)


def solution(mesh):
    size = mesh.shape["blk"]
    chips = size // 2
    order = chip_order(mesh, size)

    def step(value, shift):
        pairs = [
            (order[p] * 2 + c, order[(p + shift) % chips] * 2 + c)
            for p in range(chips)
            for c in range(2)
        ]
        return lax.ppermute(value, "blk", pairs)

    def flip(value, bit):
        return lax.ppermute(value, "blk", [(i, i ^ bit) for i in range(size)])

    def on_device(
        features,
        tiles,
        block_rows,
        block_cols,
        block_count,
        ln_gain,
        w_msg,
        w_query,
        w_key,
        w_value,
        w_gate,
        w_out,
        omega,
        ln2_gain,
        w_up,
        w_down,
    ):
        nodes, width = features.shape
        tile = tiles.shape[1]
        feat = omega.shape[1]
        head = width // HEADS
        row_blocks = nodes // tile
        me = lax.axis_index("blk")
        core = (me % 2).reshape(1)
        me = me.reshape(1)
        normed, message = call(
            message_kernel,
            (sds((nodes, width), BF16), sds((nodes, width), BF16)),
            [HBM] * 3,
            (features, ln_gain.reshape(1, width), w_msg),
            buffers((features, PIECES), (sds((1, width), F32), 1), (w_msg, PIECES)),
            EXTRA,
        )

        full = (chips - 1) // 2
        ahead, back = step(message, 1), step(message, -1)

        rows = feat + 16
        given = sds((rows, feat), BF16)
        own, near, across, both, done = call(
            kv_kernel,
            (sds((rows, feat), F32), given, given, given, sds((1,), jnp.int32)),
            [HBM] * 4,
            (normed, w_key, w_value, omega),
            [pltpu.VMEM((HEADS // 2, rows, feat), F32)]
            + buffers((normed, PIECES), (w_key, PIECES), (w_value, PIECES), (omega, 1)),
            56,
        )
        ahead, back = after([ahead, back], done)
        sums = [sum((flip(v, b).astype(F32) for v, b in ((near, 2), (across, 1), (both, 3))), own)]
        bit = 4
        while bit < size:
            hops = [3 * bit, 2 * bit, bit] if 2 * bit < size else [bit]
            sent = sums[-1].astype(BF16)
            sums.append(sum((flip(sent, hop).astype(F32) for hop in hops), sums[-1]))
            bit *= 4
        quarter = sums[-1].astype(BF16)

        qfeat, gate = call(
            query_kernel,
            (sds((nodes, HEADS * feat), BF16), sds((nodes, width), F32)),
            [VMEM] * 4,
            (normed, w_query, w_gate, omega),
        )
        blocks = sds((chips * row_blocks, row_blocks, tile, tile), BF16)
        dense, others = call(
            place_kernel,
            (blocks, blocks),
            [SMEM] * 4 + [VMEM, pl.BlockSpec(memory_space=pl.ANY)],
            (core, block_rows, block_cols, block_count, tiles, sums[0]),
        )
        shifts = [0] + [sign * k for k in range(1, full + 1) for sign in (1, -1)]
        if chips % 2 == 0:
            shifts += [chips // 2]
        home = {chip: p for p, chip in enumerate(order)}

        def lookup(values, index):
            return sum(jnp.where(index == i, value, 0) for i, value in enumerate(values))

        def accumulate(totals, first, chunks, aside=None):
            totals = list(totals)
            early = [] if aside is None else [w_up, w_down]

            def body(mine_ref, sibling_ref, *refs):
                place_here = lookup([home[c] for c in range(chips)], lax.axis_index("blk") // 2)
                chunk_refs = refs[len(totals) : len(totals) + len(chunks)]
                outs = refs[len(totals) + len(chunks) + len(early) :]

                def weights(dense_ref, place):
                    chip = lookup(order, lax.rem(place_here - shifts[place] + 2 * chips, chips))
                    return columns(dense_ref, chip * row_blocks, nodes)

                for i, dense_ref in enumerate((mine_ref, sibling_ref)):
                    value = refs[i][...] if totals else None
                    for place, chunk_ref in enumerate(chunk_refs):
                        part = dot(weights(dense_ref, first + place), chunk_ref[...])
                        value = part if value is None else value + part
                    outs[i][...] = value
                    if aside is not None:
                        outs[2 + i][...] = weights(dense_ref, aside)

            outs = [sds((nodes, width), F32)] * 2
            if aside is not None:
                outs += [sds((nodes, nodes), BF16)] * 2
            return call(
                body,
                outs,
                [VMEM] * (2 + len(totals) + len(chunks))
                + [pl.BlockSpec(memory_space=pl.ANY)] * len(early),
                (dense, sibling, *totals, *chunks, *early),
            )

        chunks = [message, ahead, back]
        totals, used = (), 0
        sibling = None
        for k in range(2, full + 1):
            if k == 3:
                ahead, back, others = after([ahead, back, others], dense)
                chunks[-2:] = [ahead, back]
                sibling = flip(others, 1)
            if k > 3:
                ready = 1 + 2 * (k - 2)
                totals = accumulate(totals, used, chunks[used:ready])
                used = ready
                ahead, back = after([ahead, back], totals[0])
                chunks[-2:] = [ahead, back]
            ahead, back = step(ahead, 1), step(back, -1)
            chunks += [ahead, back]
        ready = 1 + 2 * (full - 1)
        totals = accumulate(totals, used, chunks[used:ready])
        ahead, back = after([ahead, back], qfeat, totals[0])
        chunks[-2:] = [ahead, back]
        late = [step(ahead[: nodes // 2], 1), step(back[nodes // 2 :], -1)]
        *totals, mine_late, sibling_late = accumulate(totals, ready, chunks[ready:], len(chunks))
        gathered = [flip(quarter, bits) for bits in (2, 1, 3)]
        mixed = call(
            attend_kernel,
            sds((nodes, width), F32),
            [VMEM] * 9,
            (features, qfeat, gate, quarter, *gathered, w_out, totals[0]),
        )
        late = after(late, *totals, *gathered)
        late_given, late_mine = sds((nodes, width), BF16), sds((nodes, width), F32)
        given = call(late_kernel, late_given, [VMEM] * 4, (totals[1], sibling_late, *late))
        mine = call(late_kernel, late_mine, [VMEM] * 4, (mixed, mine_late, *late))
        theirs = flip(given, 1)

        def final_kernel(mine_ref, theirs_ref, gain_ref, up_ref, down_ref, out_ref):
            mixed = mine_ref[...] + theirs_ref[...].astype(F32)
            second = layer_norm(mixed, gain_ref[...])
            inner = jnp.maximum(dot(second, up_ref[...]), 0.0).astype(BF16)
            out_ref[...] = (mixed + dot(inner, down_ref[...])).astype(BF16)

        return call(
            final_kernel,
            sds((nodes, width), BF16),
            [VMEM] * 5,
            (mine, theirs, ln2_gain.reshape(1, width), w_up, w_down),
        )

    split_rows = P(("groups", "blk"))
    return jax.shard_map(
        on_device,
        mesh=mesh,
        in_specs=(split_rows,) * 5 + (P(),) * 11,
        out_specs=P(("groups", "blk"), None),
        check_vma=False,
    )


def chip_order(mesh, size):
    devices = mesh.devices.reshape(-1, size)[0]
    coords = [getattr(d, "coords", None) for d in devices[::2]]
    if any(c is None for c in coords) or len({c[1] for c in map(tuple, coords)}) != 2:
        return list(range(size // 2))
    low = min(c[1] for c in coords)
    up = sorted((i for i, c in enumerate(coords) if c[1] == low), key=lambda i: coords[i][2])
    down = sorted((i for i, c in enumerate(coords) if c[1] != low), key=lambda i: -coords[i][2])
    return up + down
```

```python
import jax
import jax.numpy as jnp
from jax import lax
from jax.experimental import pallas as pl
from jax.experimental.pallas import tpu as pltpu
from jax.sharding import PartitionSpec as P

HEADS = 8
EPS = 1e-05
F32 = jnp.float32
BF16 = jnp.bfloat16
VMEM = pl.BlockSpec(memory_space=pltpu.VMEM)
SMEM = pl.BlockSpec(memory_space=pltpu.SMEM)
HBM = pl.BlockSpec(memory_space=pltpu.HBM)


def dot(a, b):
    return jnp.dot(a, b, preferred_element_type=F32)


def split(value):
    high = value.astype(BF16)
    return high, (value - high.astype(F32)).astype(BF16)


def layer_norm(values, gain):
    mean = jnp.mean(values, axis=-1, keepdims=True)
    centered = values - mean
    var = jnp.mean(centered * centered, axis=-1, keepdims=True)
    return (centered * lax.rsqrt(var + EPS) * gain).astype(BF16)


def call(body, outs, specs, args, scratch=(), limit=None):
    held = sum(a.size * a.dtype.itemsize for a in (*args, *jax.tree.leaves(outs)))
    limit = limit or held // 2**20 + 7
    return pl.pallas_call(
        body,
        out_shape=outs,
        in_specs=specs,
        out_specs=jax.tree.map(lambda o: SMEM if o.shape == (1,) else VMEM, outs),
        scratch_shapes=scratch,
        compiler_params=pltpu.CompilerParams(vmem_limit_bytes=int(limit * 2**20)),
        cost_estimate=pl.CostEstimate(flops=1, bytes_accessed=1, transcendentals=0),
    )(*args)


def after(values, *others):
    any_space = pl.BlockSpec(memory_space=pl.ANY)
    return pl.pallas_call(
        lambda *refs: None,
        out_shape=[sds(v.shape, v.dtype) for v in values],
        in_specs=[SMEM if v.shape == (1,) else any_space for v in (*values, *others)],
        out_specs=[any_space] * len(values),
        input_output_aliases={i: i for i in range(len(values))},
        compiler_params=pltpu.CompilerParams(vmem_limit_bytes=2**20),
        cost_estimate=pl.CostEstimate(flops=1, bytes_accessed=1, transcendentals=0),
    )(*values, *others)


def sds(shape, dtype):
    return jax.ShapeDtypeStruct(shape, dtype)


def pair_ones(rows, lanes):
    top = lax.broadcasted_iota(jnp.int32, (rows, lanes), 0) < rows // 2
    left = lax.broadcasted_iota(jnp.int32, (rows, lanes), 1) < lanes // 2
    return jnp.where(top == left, 1.0, 0.0)


def pair_omega(omega):
    zero = jnp.zeros_like(omega)
    return jnp.concatenate(
        [jnp.concatenate([omega, zero], axis=1), jnp.concatenate([zero, omega], axis=1)], axis=0
    )


class Fetch:
    def __init__(self, source, target, sems, pieces):
        rows = source.shape[0] // pieces
        self.copies = [
            pltpu.make_async_copy(
                source.at[pl.ds(i * rows, rows)], target.at[pl.ds(i * rows, rows)], sems.at[i]
            )
            for i in range(pieces)
        ]
        for copy in self.copies:
            copy.start()

    def wait(self):
        for copy in self.copies:
            copy.wait()


def buffers(*fetches):
    return [pltpu.VMEM(a.shape, a.dtype) for a, _ in fetches] + [
        pltpu.SemaphoreType.DMA((pieces,)) for _, pieces in fetches
    ]


PIECES = 4
EXTRA = 56


def message_kernel(
    x_hbm, gain_hbm, w_hbm, normed_ref, msg_ref, x_ref, gain_ref, w_ref, x_sem, gain_sem, w_sem
):
    x_copy = Fetch(x_hbm, x_ref, x_sem, PIECES)
    gain_copy = Fetch(gain_hbm, gain_ref, gain_sem, 1)
    w_copy = Fetch(w_hbm, w_ref, w_sem, PIECES)
    gain_copy.wait()
    x_copy.wait()
    normed = layer_norm(x_ref[...].astype(F32), gain_ref[...])
    normed_ref[...] = normed
    w_copy.wait()
    msg_ref[...] = dot(normed, w_ref[...]).astype(BF16)


def kv_kernel(
    normed_hbm, wk_hbm, wv_hbm, omega_hbm, own_ref, near_ref, core_ref, both_ref, done_ref, sums_ref,
    normed_ref, wk_ref, wv_ref, omega_ref, normed_sem, wk_sem, wv_sem, omega_sem
):
    normed_copy = Fetch(normed_hbm, normed_ref, normed_sem, PIECES)
    wk_copy = Fetch(wk_hbm, wk_ref, wk_sem, PIECES)
    omega_copy = Fetch(omega_hbm, omega_ref, omega_sem, 1)
    wv_copy = Fetch(wv_hbm, wv_ref, wv_sem, PIECES)
    width = normed_ref.shape[1]
    head = width // HEADS
    feat = omega_ref.shape[1]
    normed_copy.wait()
    normed = normed_ref[...]
    wk_copy.wait()
    keys = dot(normed, wk_ref[...]) * (head ** (-0.25))
    omega_copy.wait()
    wv_copy.wait()
    values = dot(normed, wv_ref[...])
    high, low = split(pair_omega(omega_ref[...]))
    ones = (-0.5 * pair_ones(2 * head, 2 * feat)).astype(BF16)
    first = jnp.concatenate([high, high], axis=0)
    second = jnp.concatenate([low, ones, ones], axis=0)
    left = lax.broadcasted_iota(jnp.int32, (feat, 2 * head), 1) < head
    pad = jnp.zeros((own_ref.shape[0] - feat - 2, feat), F32)
    for pair in range(HEADS // 2):
        k_pair = keys[:, pair * 2 * head : (pair + 1) * 2 * head]
        k_high, k_low = split(k_pair)
        s_high, s_low = split(k_pair * k_pair)
        logits = dot(jnp.concatenate([k_high, k_low], axis=1), first) + dot(
            jnp.concatenate([k_high, s_high, s_low], axis=1), second
        )
        kfeat = jnp.exp(logits)
        total = jnp.sum(kfeat, axis=0, keepdims=True)
        f_high, f_low = split(kfeat)
        v_high, v_low = split(values[:, pair * 2 * head : (pair + 1) * 2 * head])
        dims = (((0,), (0,)), ((), ()))
        both = lax.dot_general(f_high, v_high, dims, preferred_element_type=F32)
        both += lax.dot_general(f_low, v_high, dims, preferred_element_type=F32)
        both += lax.dot_general(f_high, v_low, dims, preferred_element_type=F32)
        block = jnp.where(left, both[:feat], both[feat:])
        sums_ref[pair] = jnp.concatenate([block, total[:, :feat], total[:, feat:], pad], axis=0)
    me = lax.axis_index("blk")
    mine = (me % 2) * 2 + (me // 2) % 2
    own_ref[...] = sums_ref[mine]
    near_ref[...] = sums_ref[mine ^ 1].astype(BF16)
    core_ref[...] = sums_ref[mine ^ 2].astype(BF16)
    both_ref[...] = sums_ref[mine ^ 3].astype(BF16)
    done_ref[0] = mine


def query_kernel(normed_ref, wq_ref, wg_ref, omega_ref, qf_ref, gate_ref):
    normed = normed_ref[...]
    width = normed.shape[1]
    head = width // HEADS
    feat = omega_ref.shape[1]
    query = dot(normed, wq_ref[...]) * (head ** (-0.25))
    high, low = split(pair_omega(omega_ref[...]))
    first = jnp.concatenate([high, high], axis=0)
    for pair in range(HEADS // 2):
        q_high, q_low = split(query[:, pair * 2 * head : (pair + 1) * 2 * head])
        logits = dot(jnp.concatenate([q_high, q_low], axis=1), first) + dot(q_high, low)
        qf_ref[:, pair * 2 * feat : (pair + 1) * 2 * feat] = jnp.exp(logits).astype(BF16)
    gate_ref[...] = jax.nn.sigmoid(dot(normed, wg_ref[...]))


def place_kernel(core_ref, rows_ref, cols_ref, count_ref, tiles_ref, before_ref, mine_ref, theirs_ref):
    del before_ref
    per = mine_ref.shape[1]
    mine_ref[...] = jnp.zeros_like(mine_ref)
    theirs_ref[...] = jnp.zeros_like(theirs_ref)

    def body(slot, carry):
        col, row = cols_ref[slot], rows_ref[slot]
        place = (col // (2 * per)) * per + col % per
        own = (col // per) % 2 == core_ref[0]

        @pl.when(own)
        def _():
            mine_ref[place, row] = tiles_ref[slot]

        @pl.when(jnp.logical_not(own))
        def _():
            theirs_ref[place, row] = tiles_ref[slot]

        return carry

    lax.fori_loop(0, count_ref[0], body, 0)


def attend_kernel(
    x_ref, qf_ref, gate_ref, own_ref, pair_ref, core_ref, both_ref, wo_ref, total_ref, mixed_ref
):
    width = x_ref.shape[1]
    head = width // HEADS
    feat = own_ref.shape[1]
    me = lax.axis_index("blk")
    mine = (me % 2) * 2 + (me // 2) % 2
    left = lax.broadcasted_iota(jnp.int32, (feat, 2 * head), 1) < head
    ones = pair_ones(2 * feat, 2 * head).astype(BF16)
    joined = []
    for pair in range(HEADS // 2):
        offset = mine ^ pair
        part = own_ref[...].astype(F32)
        for other, ref in ((1, pair_ref), (2, core_ref), (3, both_ref)):
            part = jnp.where(offset == other, ref[...].astype(F32), part)
        block = part[:feat]
        block = jnp.concatenate([jnp.where(left, block, 0.0), jnp.where(left, 0.0, block)], axis=0)
        ksum = jnp.concatenate([part[feat : feat + 1], part[feat + 1 : feat + 2]], axis=1)
        q_pair = qf_ref[:, pair * 2 * feat : (pair + 1) * 2 * feat]
        numer = dot(q_pair, block.astype(BF16))
        d_high, d_low = split(q_pair.astype(F32) * ksum)
        denom = dot(d_high, ones) + dot(d_low, ones)
        joined.append(numer / denom)
    attn = jnp.concatenate(joined, axis=1)
    gated = (attn * gate_ref[...]).astype(BF16)
    mixed_ref[...] = x_ref[...].astype(F32) + total_ref[...] + dot(gated, wo_ref[...])


def columns(dense_ref, column, count):
    rows, tile = dense_ref.shape[1:3]
    weights = [
        jnp.concatenate([dense_ref[column + col, row] for col in range(count // tile)], axis=1)
        for row in range(rows)
    ]
    return jnp.concatenate(weights, axis=0)


def late_kernel(total_ref, weights_ref, upper_ref, lower_ref, out_ref):
    rows = jnp.concatenate([upper_ref[...], lower_ref[...]], axis=0)
    out_ref[...] = (total_ref[...] + dot(weights_ref[...], rows)).astype(out_ref.dtype)


def solution(mesh):
    size = mesh.shape["blk"]
    chips = size // 2
    order = chip_order(mesh, size)

    def step(value, shift):
        pairs = [
            (order[p] * 2 + c, order[(p + shift) % chips] * 2 + c)
            for p in range(chips)
            for c in range(2)
        ]
        return lax.ppermute(value, "blk", pairs)

    def flip(value, bit):
        return lax.ppermute(value, "blk", [(i, i ^ bit) for i in range(size)])

    def on_device(
        features,
        tiles,
        block_rows,
        block_cols,
        block_count,
        ln_gain,
        w_msg,
        w_query,
        w_key,
        w_value,
        w_gate,
        w_out,
        omega,
        ln2_gain,
        w_up,
        w_down,
    ):
        nodes, width = features.shape
        tile = tiles.shape[1]
        feat = omega.shape[1]
        head = width // HEADS
        row_blocks = nodes // tile
        me = lax.axis_index("blk")
        core = (me % 2).reshape(1)
        me = me.reshape(1)
        normed, message = call(
            message_kernel,
            (sds((nodes, width), BF16), sds((nodes, width), BF16)),
            [HBM] * 3,
            (features, ln_gain.reshape(1, width), w_msg),
            buffers((features, PIECES), (sds((1, width), F32), 1), (w_msg, PIECES)),
            EXTRA,
        )

        full = (chips - 1) // 2
        ahead, back = step(message, 1), step(message, -1)

        rows = feat + 16
        given = sds((rows, feat), BF16)
        own, near, across, both, done = call(
            kv_kernel,
            (sds((rows, feat), F32), given, given, given, sds((1,), jnp.int32)),
            [HBM] * 4,
            (normed, w_key, w_value, omega),
            [pltpu.VMEM((HEADS // 2, rows, feat), F32)]
            + buffers((normed, PIECES), (w_key, PIECES), (w_value, PIECES), (omega, 1)),
            56,
        )
        ahead, back = after([ahead, back], done)
        sums = [sum((flip(v, b).astype(F32) for v, b in ((near, 2), (across, 1), (both, 3))), own)]
        bit = 4
        while bit < size:
            hops = [3 * bit, 2 * bit, bit] if 2 * bit < size else [bit]
            sent = sums[-1].astype(BF16)
            sums.append(sum((flip(sent, hop).astype(F32) for hop in hops), sums[-1]))
            bit *= 4
        quarter = sums[-1].astype(BF16)

        qfeat, gate = call(
            query_kernel,
            (sds((nodes, HEADS * feat), BF16), sds((nodes, width), F32)),
            [VMEM] * 4,
            (normed, w_query, w_gate, omega),
        )
        blocks = sds((chips * row_blocks, row_blocks, tile, tile), BF16)
        dense, others = call(
            place_kernel,
            (blocks, blocks),
            [SMEM] * 4 + [VMEM, pl.BlockSpec(memory_space=pl.ANY)],
            (core, block_rows, block_cols, block_count, tiles, sums[0]),
        )
        shifts = [0] + [sign * k for k in range(1, full + 1) for sign in (1, -1)]
        if chips % 2 == 0:
            shifts += [chips // 2]
        home = {chip: p for p, chip in enumerate(order)}

        def lookup(values, index):
            return sum(jnp.where(index == i, value, 0) for i, value in enumerate(values))

        def accumulate(totals, first, chunks, aside=None):
            totals = list(totals)
            early = [] if aside is None else [w_up, w_down]

            def body(mine_ref, sibling_ref, *refs):
                place_here = lookup([home[c] for c in range(chips)], lax.axis_index("blk") // 2)
                chunk_refs = refs[len(totals) : len(totals) + len(chunks)]
                outs = refs[len(totals) + len(chunks) + len(early) :]

                def weights(dense_ref, place):
                    chip = lookup(order, lax.rem(place_here - shifts[place] + 2 * chips, chips))
                    return columns(dense_ref, chip * row_blocks, nodes)

                for i, dense_ref in enumerate((mine_ref, sibling_ref)):
                    value = refs[i][...] if totals else None
                    for place, chunk_ref in enumerate(chunk_refs):
                        part = dot(weights(dense_ref, first + place), chunk_ref[...])
                        value = part if value is None else value + part
                    outs[i][...] = value
                    if aside is not None:
                        outs[2 + i][...] = weights(dense_ref, aside)

            outs = [sds((nodes, width), F32)] * 2
            if aside is not None:
                outs += [sds((nodes, nodes), BF16)] * 2
            return call(
                body,
                outs,
                [VMEM] * (2 + len(totals) + len(chunks))
                + [pl.BlockSpec(memory_space=pl.ANY)] * len(early),
                (dense, sibling, *totals, *chunks, *early),
            )

        chunks = [message, ahead, back]
        totals, used = (), 0
        sibling = None
        for k in range(2, full + 1):
            if k == 3:
                ahead, back, others = after([ahead, back, others], dense)
                chunks[-2:] = [ahead, back]
                sibling = flip(others, 1)
            if k > 3:
                ready = 1 + 2 * (k - 2)
                totals = accumulate(totals, used, chunks[used:ready])
                used = ready
                ahead, back = after([ahead, back], totals[0])
                chunks[-2:] = [ahead, back]
            ahead, back = step(ahead, 1), step(back, -1)
            chunks += [ahead, back]
        ready = 1 + 2 * (full - 1)
        totals = accumulate(totals, used, chunks[used:ready])
        ahead, back = after([ahead, back], qfeat, totals[0])
        chunks[-2:] = [ahead, back]
        late = [step(ahead[: nodes // 2], 1), step(back[nodes // 2 :], -1)]
        *totals, mine_late, sibling_late = accumulate(totals, ready, chunks[ready:], len(chunks))
        gathered = [flip(quarter, bits) for bits in (2, 1, 3)]
        mixed = call(
            attend_kernel,
            sds((nodes, width), F32),
            [VMEM] * 9,
            (features, qfeat, gate, quarter, *gathered, w_out, totals[0]),
        )
        late = after(late, *gathered)
        late_given, late_mine = sds((nodes, width), BF16), sds((nodes, width), F32)
        given = call(late_kernel, late_given, [VMEM] * 4, (totals[1], sibling_late, *late))
        mine = call(late_kernel, late_mine, [VMEM] * 4, (mixed, mine_late, *late))
        theirs = flip(given, 1)

        def final_kernel(mine_ref, theirs_ref, gain_ref, up_ref, down_ref, out_ref):
            mixed = mine_ref[...] + theirs_ref[...].astype(F32)
            second = layer_norm(mixed, gain_ref[...])
            inner = jnp.maximum(dot(second, up_ref[...]), 0.0).astype(BF16)
            out_ref[...] = (mixed + dot(inner, down_ref[...])).astype(BF16)

        return call(
            final_kernel,
            sds((nodes, width), BF16),
            [VMEM] * 5,
            (mine, theirs, ln2_gain.reshape(1, width), w_up, w_down),
        )

    split_rows = P(("groups", "blk"))
    return jax.shard_map(
        on_device,
        mesh=mesh,
        in_specs=(split_rows,) * 5 + (P(),) * 11,
        out_specs=P(("groups", "blk"), None),
        check_vma=False,
    )


def chip_order(mesh, size):
    devices = mesh.devices.reshape(-1, size)[0]
    coords = [getattr(d, "coords", None) for d in devices[::2]]
    if any(c is None for c in coords) or len({c[1] for c in map(tuple, coords)}) != 2:
        return list(range(size // 2))
    low = min(c[1] for c in coords)
    up = sorted((i for i, c in enumerate(coords) if c[1] == low), key=lambda i: coords[i][2])
    down = sorted((i for i, c in enumerate(coords) if c[1] != low), key=lambda i: -coords[i][2])
    return up + down
```
